128 devices in a mesh: ctx: 4 (over x), head: 32 (over y, z, core).
Axes of the slice: x: 4, y: 4, z: 4, core: 2. Of those that a mesh axis runs over, the one named last changes fastest.
Arguments:
- hidden_rows: float32 [2048, 2304], P(('ctx', 'head')), may hold values from -60 to 60
- segment_ids: int32 [2048], replicated, may hold values from 0 to 1, never falling along the last dimension, each value on 1 to 1920 neighbouring positions
- w_query: float32 [2304, 6144], P(None, 'head'), may hold values from -0.125 to 0.125
- w_down: float32 [2304, 576], replicated, may hold values from -0.125 to 0.125
- w_up: float32 [512, 8192], P(None, 'head'), may hold values from -0.25 to 0.25
- w_out: float32 [4096, 2304], P('head'), may hold values from -0.09375 to 0.09375
Outputs:
- attended: float32 [2048, 2304], P(('ctx', 'head'))
- log_norm: float32 [32, 2048], P('head', 'ctx')
The draws below stay inside these ranges and needn't reach their ends.
All inputs are finite; a program needn't handle non-finite values.
Results may differ from the reference program's by a relative error of at most 0.00015.
Values sent between devices are 32-bit elements; how exact they have to be, the bound alone decides.
A program may use at most 64 MiB of HBM per device.

```python
import math
import jax
import jax.numpy as jnp
import numpy as np
from jax import lax

D = 2304
H = 32
KV_RANK = 512
NOPE = 128
ROPE = 64
VDIM = 128
TOK_CTX = 512
TOKENS = 2048


def draw_hidden_rows(key, part):
    first, second = jax.random.split(key, 2)
    row_scales = jnp.exp(jax.random.uniform(first, (TOKENS, 1), minval=-0.3, maxval=0.3))
    values = jnp.clip(jax.random.normal(second, (TOKENS, D)), -6.0, 6.0) * row_scales
    return jnp.clip(values, -60.0, 60.0).astype(jnp.float32)


def levels(rng, extent, cuts, least, high):
    def one(dim, blocks):
        heights = jax.random.uniform(jax.random.fold_in(jax.random.fold_in(rng, 6), dim), (blocks,), jnp.float32, least / len(cuts), high / len(cuts))
        return jnp.repeat(jnp.exp(heights), extent[dim] // blocks).reshape((-1,) + (1,) * (len(extent) - dim - 1))

    level = one(*cuts[0])
    for cut in cuts[1:]:
        level = level * one(*cut)
    return level


def length_profile(amount, total, reach, lean):
    weights = [(1 << 20) // math.isqrt(rank ** lean) + 1 for rank in range(2, amount + 1)]
    spare, counts = total - reach - (amount - 1), [1] * (amount - 1)
    while spare > 0:
        free = [i for i in range(amount - 1) if counts[i] < reach]
        whole, left = sum([weights[i] for i in free]), spare
        for i in free:
            addition = min(reach - counts[i], max(1, left * weights[i] // whole), spare)
            counts[i] = counts[i] + addition
            spare = spare - addition
    return np.array([reach] + counts)


def uneven_parts(rng, amount, total, most, lean):
    if amount == 2:
        one = jax.random.randint(rng, (), max(1, total - most), min(most, total - 1) + 1)
        return jnp.stack([one, total - one])
    tallies = jnp.asarray(length_profile(amount, total, most, lean), jnp.int32)
    pairs = (amount - 1) // 2
    giver, receiver = tallies[1:1 + 2 * pairs:2], tallies[2:2 + 2 * pairs:2]
    slack = jnp.minimum(giver - 1, most - receiver)
    passed = jax.random.randint(jax.random.fold_in(rng, 1), (pairs,), 0, 1 << 20) % (slack + 1)
    tallies = tallies.at[1:1 + 2 * pairs:2].set(giver - passed).at[2:2 + 2 * pairs:2].set(receiver + passed)
    return tallies[jax.random.permutation(jax.random.fold_in(rng, 2), amount)]


def scatter_about(stream_key, dims, spread, most, pieces=(), held_as=jnp.bfloat16):
    array = spread * jax.random.normal(stream_key, dims, jnp.float32)
    if pieces:
        array = array * levels(stream_key, dims, pieces, -0.22, 0.18)
    return jnp.clip(array, -most, most).astype(held_as)


def setup_inputs(seed: int = 0) -> dict:
    seeds = jax.random.split(jax.random.key(seed), 7)
    hidden_rows = draw_hidden_rows(jax.random.fold_in(seeds[6], 71), 0)
    segment_ids = jnp.searchsorted(jnp.cumsum(uneven_parts(seeds[1], 2, TOKENS, TOKENS - TOK_CTX // 4, 0)), jnp.arange(TOKENS), side="right").astype(jnp.int32)
    w_query = scatter_about(seeds[2], (D, H * (NOPE + ROPE)), D ** -0.5, 0.125, ((1, 32),), jnp.float32)
    w_down = scatter_about(seeds[3], (D, KV_RANK + ROPE), D ** -0.5, 0.125, (), jnp.float32)
    w_up = scatter_about(seeds[4], (KV_RANK, H * (NOPE + VDIM)), KV_RANK ** -0.5, 0.25, ((1, 32),), jnp.float32)
    w_out = scatter_about(seeds[5], (H * VDIM, D), (H * VDIM) ** -0.5, 0.09375, ((0, 32),), jnp.float32)
    return {"hidden_rows": hidden_rows, "segment_ids": segment_ids, "w_query": w_query, "w_down": w_down, "w_up": w_up, "w_out": w_out}


eps_norm = 1e-06
neg_fill = -1e+30
precise = lax.Precision.HIGHEST

def product(left, right):
    return jnp.dot(left, right, precision=precise, preferred_element_type=jnp.float32)

def normalize(raw_latent):
    compressed = raw_latent[:, :KV_RANK]
    mean_square = lax.optimization_barrier(jnp.mean(compressed * compressed, axis=1, keepdims=True))
    return jnp.concatenate([compressed * lax.rsqrt(mean_square + eps_norm), raw_latent[:, KV_RANK:]], axis=1)

def reference(hidden_rows, segment_ids, w_query, w_down, w_up, w_out):
    queries = product(hidden_rows, w_query).reshape(TOKENS, H, NOPE + ROPE).transpose(1, 0, 2)
    latent = normalize(product(hidden_rows, w_down))
    up_proj = product(latent[:, :KV_RANK], w_up).reshape(TOKENS, H, NOPE + VDIM).transpose(1, 0, 2)
    shared = latent[:, KV_RANK:]
    positions = jnp.arange(TOKENS, dtype=jnp.int32)
    allowed = (positions[None, :] <= positions[:, None]) & (segment_ids[None, :] == segment_ids[:, None])
    score_factor = 1.0 / math.sqrt(NOPE + ROPE)

    def per_head(operands):
        head_query, head_up = operands
        keys = jnp.concatenate([head_up[:, :NOPE], shared], axis=1)
        scores = jnp.dot(head_query, keys.T, precision=precise, preferred_element_type=jnp.float32) * score_factor
        scores = jnp.where(allowed, scores, neg_fill)
        peak = lax.optimization_barrier(jnp.max(scores, axis=1))
        weights = jnp.where(allowed, jnp.exp(scores - peak[:, None]), 0.0)
        total = lax.optimization_barrier(jnp.sum(weights, axis=1))
        result = product(weights, head_up[:, NOPE:]) / total[:, None]
        return (result, peak + jnp.log(total))
    outputs, log_norm = lax.map(per_head, (queries, up_proj))
    flattened = outputs.transpose(1, 0, 2).reshape(TOKENS, H * VDIM)
    return (product(flattened, w_out), log_norm)
```

```python
import functools
import math

import jax
import jax.numpy as jnp
from jax import lax
from jax.experimental import pallas as pl
from jax.experimental.pallas import tpu as pltpu
from jax.sharding import PartitionSpec as P

D = 2304
KV_RANK = 512
NOPE = 128
ROPE = 64
VDIM = 128
QK = NOPE + ROPE
TOK_CTX = 512
LAT = 640
HALF = D // 2

eps_norm = 1e-06
neg_fill = -1e30
f32 = jnp.float32
bf16 = jnp.bfloat16
MESH = pl.DeviceIdType.MESH
N_SEM = 160


def split(value):
    high = value.astype(bf16)
    return high, (value - high.astype(f32)).astype(bf16)


def dot(left, right, dims=((1,), (0,))):
    return lax.dot_general(left, right, (dims, ((), ())), preferred_element_type=f32)


def dot3(left, right, dims=((1,), (0,))):
    (left_high, left_low), (right_high, right_low) = left, right
    small = dot(left_high, right_low, dims) + dot(left_low, right_high, dims)
    return dot(left_high, right_high, dims) + small


def kernel(
    x_in, seg_in, wq_in, wd_in, wu_in, wo_in,
    out, ln_out,
    xs, lat, wq, wd, wu, wo, kv, kv_far, qh, ql, accq,
    top, tot, acc, part, relay, sums, relay2, sums2, red, ln, ln_far,
    send_sem, recv_sem, load_sem,
):
    ctx = lax.axis_index("ctx")
    head = lax.axis_index("head")
    core = lax.rem(head, 2)
    z0 = lax.rem(lax.div(head, 2), 4)
    y0 = lax.div(head, 8)

    def at(y, z):
        return (ctx, (y * 4 + z) * 2 + core)

    def turn(i, by):
        return lax.rem(i + by + 4, 4)

    ym, yp, yo = turn(y0, -1), turn(y0, 1), turn(y0, 2)
    zm, zp, zo = turn(z0, -1), turn(z0, 1), turn(z0, 2)
    Y_UP, Y_DOWN = at(yp, z0), at(ym, z0)
    Z_UP, Z_DOWN = at(y0, zp), at(y0, zm)
    PARTNER = (ctx, head + 1 - 2 * core)
    X_PEERS = [(turn(ctx, by), head) for by in (1, 2, 3)]

    barrier = pltpu.get_barrier_semaphore()
    peers = [Y_UP, Y_DOWN, Z_UP, Z_DOWN, PARTNER] + X_PEERS
    for peer in peers:
        pl.semaphore_signal(barrier, inc=1, device_id=peer, device_id_type=MESH)

    loads = []

    def load(src, dst):
        copy = pltpu.make_async_copy(src, dst, load_sem.at[len(loads)])
        copy.start()
        loads.append(copy)
        return copy

    load_x = load(x_in, xs.at[y0, z0])
    WD_STEPS = 3
    wd_rows = D // WD_STEPS
    load_wd = [
        load(wd_in.at[pl.ds(i * wd_rows, wd_rows)], wd.at[pl.ds(i * wd_rows, wd_rows)])
        for i in range(WD_STEPS)
    ]
    load_rest = [
        load(wq_in, wq.at[core]), load(wu_in, wu.at[core]), load(wo_in, wo.at[core])
    ]
    pl.semaphore_wait(barrier, len(peers))

    copies = []

    def send(src, dst, device):
        k = len(copies)
        copy = pltpu.make_async_remote_copy(
            src_ref=src, dst_ref=dst, send_sem=send_sem.at[k], recv_sem=recv_sem.at[k],
            device_id=device, device_id_type=MESH,
        )
        copy.start()
        copies.append(copy)
        return copy

    def gather(view, own=None):
        def hand(y, z, p, h, device):
            return send(view(y, z, p, h), view(y, z, p, h), device)

        first = view(y0, z0, None, None) if own is None else own
        target = view(y0, z0, None, None)
        y1 = send(first, target, Y_UP)
        y2 = send(first, target, Y_DOWN)
        z1 = send(first, target, Z_UP)
        z2 = send(first, target, Z_DOWN)
        yield
        y1.wait_recv()
        f1 = hand(ym, z0, None, 0, Y_UP)
        a = [hand(ym, z0, 0, None, Z_UP), hand(ym, z0, 0, None, Z_DOWN)]
        z1.wait_recv()
        g1 = hand(y0, zm, None, 0, Z_UP)
        b = [hand(y0, zm, 1, None, Y_UP), hand(y0, zm, 1, None, Y_DOWN)]
        y2.wait_recv()
        f2 = hand(yp, z0, None, 1, Y_DOWN)
        a += [hand(yp, z0, 0, None, Z_UP), hand(yp, z0, 0, None, Z_DOWN)]
        z2.wait_recv()
        g2 = hand(y0, zp, None, 1, Z_DOWN)
        b += [hand(y0, zp, 1, None, Y_UP), hand(y0, zp, 1, None, Y_DOWN)]
        yield
        f1.wait_recv()
        f2.wait_recv()
        a += [hand(yo, z0, 0, None, Z_UP), hand(yo, z0, 0, None, Z_DOWN)]
        g1.wait_recv()
        g2.wait_recv()
        b += [hand(y0, zo, 1, None, Y_UP), hand(y0, zo, 1, None, Y_DOWN)]
        yield
        last = []
        for i, (y, z) in enumerate(((ym, zm), (yp, zp), (yo, zo))):
            a[2 * i].wait_recv()
            last.append(hand(y, zm, 0, 0, Z_UP))
            b[2 * i].wait_recv()
            last.append(hand(ym, z, 1, 0, Y_UP))
            a[2 * i + 1].wait_recv()
            last.append(hand(y, zp, 0, 1, Z_DOWN))
            b[2 * i + 1].wait_recv()
            last.append(hand(yp, z, 1, 1, Y_DOWN))
        yield
        for copy in last:
            copy.wait_recv()
        yield

    everything = slice(None)

    def x_view(y, z, p, h):
        cols = everything if p is None else pl.ds(p * HALF, HALF)
        return xs.at[y, z, :, :, cols] if h is None else xs.at[y, z, h, :, cols]

    def lat_view(y, z, p, h):
        return lat.at[y, z, everything if p is None else p, everything if h is None else h]

    gather_x = gather(x_view, x_in)
    next(gather_x)
    load_x.wait()
    weight_copies = [
        send(wq_in, wq.at[core], PARTNER),
        send(wu_in, wu.at[core], PARTNER),
        send(wo_in, wo.at[core], PARTNER),
    ]

    own_high, own_low = split(xs[y0, z0].reshape(16, D))
    own_both = jnp.concatenate([own_high, own_low], axis=0)
    raw2 = jnp.zeros((32, KV_RANK + ROPE), f32)
    raw1 = jnp.zeros((16, KV_RANK + ROPE), f32)
    for i in range(WD_STEPS):
        load_wd[i].wait()
        w_high, w_low = split(wd[pl.ds(i * wd_rows, wd_rows), :])
        cols = slice(i * wd_rows, (i + 1) * wd_rows)
        raw2 = raw2 + dot(own_both[:, cols], w_high)
        raw1 = raw1 + dot(own_high[:, cols], w_low)
        if i == 0:
            next(gather_x)
    raw = raw2[:16] + (raw2[16:] + raw1)
    squeezed = raw[:, :KV_RANK]
    mean_square = jnp.mean(squeezed * squeezed, axis=1, keepdims=True)
    c_hi, c_lo = lax.div(ctx, 2), lax.rem(ctx, 2)
    lat[y0, z0, c_hi, c_lo, :, pl.ds(0, KV_RANK)] = squeezed * lax.rsqrt(mean_square + eps_norm)
    lat[y0, z0, c_hi, c_lo, :, pl.ds(KV_RANK, 128)] = jnp.concatenate(
        [raw[:, KV_RANK:], jnp.zeros((16, 64), f32)], axis=1
    )
    own_lat = lat.at[y0, z0, c_hi, c_lo]
    across = [send(own_lat, own_lat, peer) for peer in X_PEERS]
    next(gather_x)
    for copy in across:
        copy.wait_recv()
    gather_lat = gather(lat_view)
    next(gather_lat)
    next(gather_x)
    next(gather_lat)
    next(gather_x)
    next(gather_lat)

    for copy in load_rest:
        copy.wait()
    for copy in weight_copies:
        copy.wait_recv()

    accq[...] = jnp.zeros_like(accq)

    def query_columns(k, carry):
        cols = pl.ds(pl.multiple_of(k * 256, 256), 256)
        rows = split(xs[:, :, :, :, cols].reshape(256, 256))
        for h in range(2):
            accq[h] += dot3(rows, split(wq[h, cols, :]))
        return carry

    lax.fori_loop(0, 4, query_columns, 0)
    next(gather_lat)
    lax.fori_loop(4, D // 256, query_columns, 0)

    for h in range(2):
        qh[h], ql[h] = split(accq[h] * (1.0 / math.sqrt(QK)))

    ones = jnp.sum(seg_in[...], axis=(0, 1), keepdims=True)
    bound = 2048 - ones
    lane = lax.broadcasted_iota(jnp.int32, (1, 256), 1)
    q_pos = ctx * TOK_CTX + lax.div(lane, 16) * 32 + core * 16 + lax.rem(lane, 16)
    q_start = jnp.where(q_pos >= bound, bound, 0)
    row = lax.broadcasted_iota(jnp.int32, (128, 1), 0)
    row_block, row_ctx, row_in = lax.div(row, 32), lax.rem(lax.div(row, 16), 2), lax.rem(row, 16)

    top[...] = jnp.full_like(top, neg_fill)
    tot[...] = jnp.zeros_like(tot)
    acc[...] = jnp.zeros_like(acc)

    def attend(block, y, z, side):
        pos_a = row_ctx * TOK_CTX + (row_block * 4 + z) * 32 + row_in + side * 16
        pos_b = (row_ctx + 2) * TOK_CTX + (y * 4 + row_block) * 32 + row_in + side * 16
        k_pos = jnp.concatenate([pos_a, pos_b], axis=0)
        allowed = (k_pos <= q_pos) & (k_pos >= q_start)
        for h in range(2):
            keys = jnp.concatenate(
                [block[:, h * 256 : h * 256 + NOPE], block[:, 512 : 512 + ROPE]], axis=1
            )
            scores = dot3(split(keys), (qh[h], ql[h]), ((1,), (1,)))
            scores = jnp.where(allowed, scores, neg_fill)
            old = top[h]
            new = jnp.maximum(old, jnp.max(scores, axis=0, keepdims=True))
            weights = jnp.where(allowed, jnp.exp(scores - new), 0.0)
            factor = jnp.exp(old - new)
            top[h] = new
            tot[h] = tot[h] * factor + jnp.sum(weights, axis=0, keepdims=True)
            values = block[:, h * 256 + NOPE : (h + 1) * 256].T
            acc[h] = acc[h] * factor + dot3(split(values), split(weights))

    def make(g, y, z):
        block_a = lat[:, z, 0].reshape(128, LAT)
        block_b = lat[y, :, 1].reshape(128, LAT)
        block = jnp.concatenate([block_a, block_b], axis=0)
        both = split(block[:, :KV_RANK])
        for h in range(2):
            kv[g, :, pl.ds(h * 256, 256)] = dot3(both, split(wu[h]))
        kv[g, :, pl.ds(512, 128)] = block[:, KV_RANK:]
        return send(kv.at[g], kv_far.at[g], PARTNER)

    first = make(0, y0, z0)
    attend(kv[0], y0, z0, core)
    first.wait_recv()
    attend(kv_far[0], y0, z0, 1 - core)
    steps = [make(1, ym, zm), make(2, yp, zp)]
    for g, (y, z) in ((1, (ym, zm)), (2, (yp, zp))):
        attend(kv[g], y, z, core)
        steps[g - 1].wait_recv()
        attend(kv_far[g], y, z, 1 - core)
    next(gather_lat)
    final = make(3, yo, zo)
    attend(kv[3], yo, zo, core)
    final.wait_recv()
    attend(kv_far[3], yo, zo, 1 - core)

    heads = []
    for h in range(2):
        ln[h] = jnp.broadcast_to(top[h] + jnp.log(tot[h]), (8, 256))
        heads.append(acc[h] / tot[h])
    ln_copy = send(ln.at[1 - core], ln_far, PARTNER)
    rows = split(jnp.concatenate(heads, axis=0).T)

    axes = (((zm, z0, zp, zo), Z_DOWN, Z_UP), ((ym, y0, yp, yo), Y_DOWN, Y_UP))

    def blocks(p, u, v):
        cols = pl.ds(p * HALF, HALF)
        return part.at[v, u, :, :, cols] if p == 0 else part.at[u, v, :, :, cols]

    low, high = pl.ds(0, 2), pl.ds(2, 2)
    waits = []
    for p in range(2):
        (um, u0, up, uo), down, upward = axes[p]
        tile = HALF // 3
        for t in range(3):
            cols = pl.ds(p * HALF + t * tile, tile)
            w_out = split(wo[:, :, cols].reshape(256, tile))
            part[:, :, :, :, cols] = dot3(rows, w_out).reshape(4, 4, 2, 8, tile)
        waits.append([
            send(blocks(p, uo, low), relay.at[p, 0], upward),
            send(blocks(p, uo, high), relay.at[p, 1], down),
            send(blocks(p, up, high), sums.at[p, 0, high], upward),
            send(blocks(p, um, low), sums.at[p, 1, low], down),
        ])
    for p in range(2):
        (um, u0, up, uo), down, upward = axes[p]
        waits[p][0].wait_recv()
        blocks(p, up, low)[...] += relay[p, 0]
        waits[p].append(send(blocks(p, up, low), sums.at[p, 0, low], upward))
        waits[p][1].wait_recv()
        blocks(p, um, high)[...] += relay[p, 1]
        waits[p].append(send(blocks(p, um, high), sums.at[p, 1, high], down))
    waits2 = []
    for p in range(2):
        (um, u0, up, uo), down, upward = axes[1 - p]
        for copy in waits[p][2:]:
            copy.wait_recv()
        red[p] = blocks(p, axes[p][0][1], pl.ds(0, 4))[...] + (sums[p, 0] + sums[p, 1])
        waits2.append([
            send(red.at[p, uo, 0], relay2.at[p, 0], upward),
            send(red.at[p, uo, 1], relay2.at[p, 1], down),
            send(red.at[p, up, 1], sums2.at[p, 0, 1], upward),
            send(red.at[p, um, 0], sums2.at[p, 1, 0], down),
        ])
    for p in range(2):
        (um, u0, up, uo), down, upward = axes[1 - p]
        waits2[p][0].wait_recv()
        red[p, up, 0] += relay2[p, 0]
        waits2[p].append(send(red.at[p, up, 0], sums2.at[p, 0, 0], upward))
        waits2[p][1].wait_recv()
        red[p, um, 1] += relay2[p, 1]
        waits2[p].append(send(red.at[p, um, 1], sums2.at[p, 1, 1], down))
    ln_copy.wait_recv()
    ln_out[core] = ln[core]
    ln_out[1 - core] = ln_far[...]
    for p in range(2):
        for copy in waits2[p][2:]:
            copy.wait_recv()
        out[:, :, pl.ds(p * HALF, HALF)] = red[p, axes[1 - p][0][1]] + (sums2[p, 0] + sums2[p, 1])
    for copy in copies:
        copy.wait_send()


def body(hidden_rows, segment_ids, w_query, w_down, w_up, w_out):
    any_space = pl.BlockSpec(memory_space=pl.ANY)
    vmem = pl.BlockSpec(memory_space=pltpu.VMEM)
    out, ln = pl.pallas_call(
        kernel,
        out_shape=(
            jax.ShapeDtypeStruct((2, 8, D), f32),
            jax.ShapeDtypeStruct((2, 8, 256), f32),
        ),
        in_specs=[any_space, vmem, any_space, any_space, any_space, any_space],
        out_specs=(vmem, vmem),
        scratch_shapes=[
            pltpu.VMEM((4, 4, 2, 8, D), f32),
            pltpu.VMEM((4, 4, 2, 2, 16, LAT), f32),
            pltpu.VMEM((2, D, QK), f32),
            pltpu.VMEM((D, KV_RANK + ROPE), f32),
            pltpu.VMEM((2, KV_RANK, 256), f32),
            pltpu.VMEM((2, VDIM, D), f32),
            pltpu.VMEM((4, 256, LAT), f32),
            pltpu.VMEM((4, 256, LAT), f32),
            pltpu.VMEM((2, 256, QK), bf16),
            pltpu.VMEM((2, 256, QK), bf16),
            pltpu.VMEM((2, 256, QK), f32),
            pltpu.VMEM((2, 1, 256), f32),
            pltpu.VMEM((2, 1, 256), f32),
            pltpu.VMEM((2, VDIM, 256), f32),
            pltpu.VMEM((4, 4, 2, 8, D), f32),
            pltpu.VMEM((2, 2, 2, 2, 8, HALF), f32),
            pltpu.VMEM((2, 2, 4, 2, 8, HALF), f32),
            pltpu.VMEM((2, 2, 8, HALF), f32),
            pltpu.VMEM((2, 2, 2, 8, HALF), f32),
            pltpu.VMEM((2, 4, 2, 8, HALF), f32),
            pltpu.VMEM((2, 8, 256), f32),
            pltpu.VMEM((8, 256), f32),
            pltpu.SemaphoreType.DMA((N_SEM,)),
            pltpu.SemaphoreType.DMA((N_SEM,)),
            pltpu.SemaphoreType.DMA((8,)),
        ],
        compiler_params=pltpu.CompilerParams(
            collective_id=0, has_side_effects=True, vmem_limit_bytes=58 * 1024 * 1024
        ),
        name="latent_attention",
    )(
        hidden_rows.reshape(2, 8, D), segment_ids.reshape(16, 128),
        w_query, w_down, w_up, w_out,
    )
    log_norm = ln[:, 0, :].reshape(2, 16, 16).transpose(1, 0, 2).reshape(1, TOK_CTX)
    return out.reshape(16, D), log_norm


def solution(mesh):
    in_specs = (
        P(("ctx", "head"), None),
        P(),
        P(None, "head"),
        P(),
        P(None, "head"),
        P("head", None),
    )
    out_specs = (P(("ctx", "head"), None), P("head", "ctx"))
    return jax.shard_map(body, mesh=mesh, in_specs=in_specs, out_specs=out_specs, check_vma=False)
```

```python
import functools
import math

import jax
import jax.numpy as jnp
from jax import lax
from jax.experimental import pallas as pl
from jax.experimental.pallas import tpu as pltpu
from jax.sharding import PartitionSpec as P

D = 2304
KV_RANK = 512
NOPE = 128
ROPE = 64
VDIM = 128
QK = NOPE + ROPE
TOK_CTX = 512
LAT = 640
HALF = D // 2

eps_norm = 1e-06
neg_fill = -1e30
f32 = jnp.float32
bf16 = jnp.bfloat16
MESH = pl.DeviceIdType.MESH
N_SEM = 160


def split(value):
    high = value.astype(bf16)
    return high, (value - high.astype(f32)).astype(bf16)


def dot(left, right, dims=((1,), (0,))):
    return lax.dot_general(left, right, (dims, ((), ())), preferred_element_type=f32)


def dot3(left, right, dims=((1,), (0,))):
    (left_high, left_low), (right_high, right_low) = left, right
    small = dot(left_high, right_low, dims) + dot(left_low, right_high, dims)
    return dot(left_high, right_high, dims) + small


def kernel(
    x_in, seg_in, wq_in, wd_in, wu_in, wo_in,
    out, ln_out,
    xs, lat, wq, wd, wu, wo, kv, kv_far, qh, ql, accq,
    top, tot, acc, part, relay, sums, sums2, red, ln, ln_far,
    send_sem, recv_sem, load_sem,
):
    ctx = lax.axis_index("ctx")
    head = lax.axis_index("head")
    core = lax.rem(head, 2)
    z0 = lax.rem(lax.div(head, 2), 4)
    y0 = lax.div(head, 8)

    def at(y, z):
        return (ctx, (y * 4 + z) * 2 + core)

    def turn(i, by):
        return lax.rem(i + by + 4, 4)

    ym, yp, yo = turn(y0, -1), turn(y0, 1), turn(y0, 2)
    zm, zp, zo = turn(z0, -1), turn(z0, 1), turn(z0, 2)
    Y_UP, Y_DOWN = at(yp, z0), at(ym, z0)
    Z_UP, Z_DOWN = at(y0, zp), at(y0, zm)
    Y_OPP, Z_OPP = at(yo, z0), at(y0, zo)
    PARTNER = (ctx, head + 1 - 2 * core)
    X_PEERS = [(turn(ctx, by), head) for by in (1, 2, 3)]

    barrier = pltpu.get_barrier_semaphore()
    peers = [Y_UP, Y_DOWN, Z_UP, Z_DOWN, Y_OPP, Z_OPP, PARTNER] + X_PEERS
    for peer in peers:
        pl.semaphore_signal(barrier, inc=1, device_id=peer, device_id_type=MESH)

    loads = []

    def load(src, dst):
        copy = pltpu.make_async_copy(src, dst, load_sem.at[len(loads)])
        copy.start()
        loads.append(copy)
        return copy

    load_x = load(x_in, xs.at[y0, z0])
    WD_STEPS = 3
    wd_rows = D // WD_STEPS
    load_wd = [
        load(wd_in.at[:, pl.ds(i * wd_rows, wd_rows)], wd.at[:, pl.ds(i * wd_rows, wd_rows)])
        for i in range(WD_STEPS)
    ]
    load_rest = [
        load(wq_in, wq.at[core]), load(wu_in, wu.at[core]), load(wo_in, wo.at[core])
    ]
    pl.semaphore_wait(barrier, len(peers))

    copies = []

    def send(src, dst, device):
        k = len(copies)
        copy = pltpu.make_async_remote_copy(
            src_ref=src, dst_ref=dst, send_sem=send_sem.at[k], recv_sem=recv_sem.at[k],
            device_id=device, device_id_type=MESH,
        )
        copy.start()
        copies.append(copy)
        return copy

    def gather(view, own=None):
        def hand(y, z, p, h, device):
            return send(view(y, z, p, h), view(y, z, p, h), device)

        first = view(y0, z0, None, None) if own is None else own
        near = [
            send(first, view(y0, z0, None, None), device)
            for device in (Y_UP, Z_UP, Y_DOWN, Z_DOWN, Y_OPP, Z_OPP)
        ]
        yield
        a, b = [], []
        for k, i, j in ((0, ym, zm), (2, yp, zp)):
            near[k].wait_recv()
            a += [hand(i, z0, 0, None, Z_UP), hand(i, z0, 0, None, Z_DOWN)]
            near[k + 1].wait_recv()
            b += [hand(y0, j, 1, None, Y_UP), hand(y0, j, 1, None, Y_DOWN)]
        yield
        near[4].wait_recv()
        a += [hand(yo, z0, 0, None, Z_UP), hand(yo, z0, 0, None, Z_DOWN)]
        near[5].wait_recv()
        b += [hand(y0, zo, 1, None, Y_UP), hand(y0, zo, 1, None, Y_DOWN)]
        yield
        last = []
        for i, (y, z) in enumerate(((ym, zm), (yp, zp), (yo, zo))):
            a[2 * i].wait_recv()
            last.append(hand(y, zm, 0, 0, Z_UP))
            b[2 * i].wait_recv()
            last.append(hand(ym, z, 1, 0, Y_UP))
            a[2 * i + 1].wait_recv()
            last.append(hand(y, zp, 0, 1, Z_DOWN))
            b[2 * i + 1].wait_recv()
            last.append(hand(yp, z, 1, 1, Y_DOWN))
        yield
        for copy in last:
            copy.wait_recv()
        yield

    everything = slice(None)

    def x_view(y, z, p, h):
        cols = everything if p is None else pl.ds(p * HALF, HALF)
        return xs.at[y, z, :, :, cols] if h is None else xs.at[y, z, h, :, cols]

    def lat_view(y, z, p, h):
        return lat.at[y, z, everything if p is None else p, everything if h is None else h]

    gather_x = gather(x_view, x_in)
    next(gather_x)
    load_x.wait()
    weight_copies = [
        send(wq_in, wq.at[core], PARTNER),
        send(wu_in, wu.at[core], PARTNER),
        send(wo_in, wo.at[core], PARTNER),
    ]

    own_high, own_low = split(xs[y0, z0].reshape(16, D))
    own_both = jnp.concatenate([own_high, own_low], axis=0)
    raw2 = jnp.zeros((32, KV_RANK + ROPE), f32)
    raw1 = jnp.zeros((16, KV_RANK + ROPE), f32)
    for i in range(WD_STEPS):
        load_wd[i].wait()
        w_high, w_low = split(wd[:, pl.ds(i * wd_rows, wd_rows)])
        cols = slice(i * wd_rows, (i + 1) * wd_rows)
        raw2 = raw2 + dot(own_both[:, cols], w_high, ((1,), (1,)))
        raw1 = raw1 + dot(own_high[:, cols], w_low, ((1,), (1,)))
        if i == 0:
            next(gather_x)
    raw = raw2[:16] + (raw2[16:] + raw1)
    squeezed = raw[:, :KV_RANK]
    mean_square = jnp.mean(squeezed * squeezed, axis=1, keepdims=True)
    c_hi, c_lo = lax.div(ctx, 2), lax.rem(ctx, 2)
    squeezed = squeezed * lax.rsqrt(mean_square + eps_norm)
    for j in range(4):
        tiles = squeezed[:, j * 128 : (j + 1) * 128].reshape(2, 8, 128)
        lat[y0, z0, c_hi, c_lo, pl.ds(2 * j, 2)] = tiles
    lat[y0, z0, c_hi, c_lo, 8] = jnp.concatenate([raw[:8, KV_RANK:], raw[8:, KV_RANK:]], axis=1)
    own_lat = lat.at[y0, z0, c_hi, c_lo]
    across = [send(own_lat, own_lat, peer) for peer in X_PEERS]
    next(gather_x)
    for copy in across:
        copy.wait_recv()
    gather_lat = gather(lat_view)
    next(gather_lat)
    next(gather_x)
    next(gather_lat)
    next(gather_x)
    next(gather_lat)

    for copy in load_rest:
        copy.wait()
    for copy in weight_copies:
        copy.wait_recv()

    accq[...] = jnp.zeros_like(accq)

    def query_columns(k, carry):
        cols = pl.ds(pl.multiple_of(k * 256, 256), 256)
        rows = split(xs[:, :, :, :, cols].reshape(256, 256))
        for h in range(2):
            accq[h] += dot3(rows, split(wq[h, :, cols]), ((1,), (1,)))
        return carry

    lax.fori_loop(0, 4, query_columns, 0)
    next(gather_lat)
    lax.fori_loop(4, D // 256, query_columns, 0)

    for h in range(2):
        qh[h], ql[h] = split(accq[h] * (1.0 / math.sqrt(QK)))

    ones = jnp.sum(seg_in[...], axis=(0, 1), keepdims=True)
    bound = 2048 - ones
    lane = lax.broadcasted_iota(jnp.int32, (1, 256), 1)
    q_pos = ctx * TOK_CTX + lax.div(lane, 16) * 32 + core * 16 + lax.rem(lane, 16)
    q_start = jnp.where(q_pos >= bound, bound, 0)
    row = lax.broadcasted_iota(jnp.int32, (128, 1), 0)
    row_block, row_ctx, row_in = lax.div(row, 32), lax.rem(lax.div(row, 16), 2), lax.rem(row, 16)

    top[...] = jnp.full_like(top, neg_fill)
    tot[...] = jnp.zeros_like(tot)
    acc[...] = jnp.zeros_like(acc)

    def attend(block, y, z, side):
        pos_a = row_ctx * TOK_CTX + (row_block * 4 + z) * 32 + row_in + side * 16
        pos_b = (row_ctx + 2) * TOK_CTX + (y * 4 + row_block) * 32 + row_in + side * 16
        k_pos = jnp.concatenate([pos_a, pos_b], axis=0)
        allowed = (k_pos <= q_pos) & (k_pos >= q_start)
        for h in range(2):
            keys = jnp.concatenate(
                [block[:, h * 256 : h * 256 + NOPE], block[:, 512 : 512 + ROPE]], axis=1
            )
            scores = dot3(split(keys), (qh[h], ql[h]), ((1,), (1,)))
            scores = jnp.where(allowed, scores, neg_fill)
            old = top[h]
            new = jnp.maximum(old, jnp.max(scores, axis=0, keepdims=True))
            weights = jnp.where(allowed, jnp.exp(scores - new), 0.0)
            factor = jnp.exp(old - new)
            top[h] = new
            tot[h] = tot[h] * factor + jnp.sum(weights, axis=0, keepdims=True)
            values = block[:, h * 256 + NOPE : (h + 1) * 256].T
            acc[h] = acc[h] * factor + dot3(split(values), split(weights))

    def make(g, y, z):
        def columns(tiles):
            pair = [lat[:, z, 0, :, tiles], lat[y, :, 1, :, tiles]]
            return jnp.concatenate([value.reshape(-1, 128) for value in pair], axis=0)

        both = split(jnp.concatenate([columns(pl.ds(2 * j, 2)) for j in range(4)], axis=1))
        for h in range(2):
            kv[g, :, pl.ds(h * 256, 256)] = dot3(both, split(wu[h]))
        shared = columns(8).reshape(16, 8, 128)
        shared = jnp.concatenate([shared[:, :, :64], shared[:, :, 64:]], axis=1).reshape(256, 64)
        kv[g, :, pl.ds(512, 64)] = shared
        kv[g, :, pl.ds(576, 64)] = jnp.zeros((256, 64), f32)
        return send(kv.at[g], kv_far.at[g], PARTNER)

    first = make(0, y0, z0)
    attend(kv[0], y0, z0, core)
    first.wait_recv()
    attend(kv_far[0], y0, z0, 1 - core)
    steps = [make(1, ym, zm), make(2, yp, zp)]
    for g, (y, z) in ((1, (ym, zm)), (2, (yp, zp))):
        attend(kv[g], y, z, core)
        steps[g - 1].wait_recv()
        attend(kv_far[g], y, z, 1 - core)
    next(gather_lat)
    final = make(3, yo, zo)
    attend(kv[3], yo, zo, core)
    final.wait_recv()
    attend(kv_far[3], yo, zo, 1 - core)

    heads = []
    for h in range(2):
        ln[h] = jnp.broadcast_to(top[h] + jnp.log(tot[h]), (8, 256))
        heads.append(acc[h] / tot[h])
    ln_copy = send(ln.at[1 - core], ln_far, PARTNER)
    rows = split(jnp.concatenate(heads, axis=0).T)

    on_z = ((zm, z0, zp, zo), Z_DOWN, Z_UP, Z_OPP)
    on_y = ((ym, y0, yp, yo), Y_DOWN, Y_UP, Y_OPP)
    axes = (on_z, on_y)

    def order(p):
        vm, v0, vp, vo = axes[1 - p][0]
        return vo, vm, vp, v0

    def rows_of(p, u, i, h):
        cols = pl.ds(p * HALF, HALF)
        v = order(p)[i]
        return part.at[v, u, h, :, cols] if p == 0 else part.at[u, v, h, :, cols]

    relays, direct, second, final2 = {}, {}, {}, {}
    for p in range(2):
        (um, u0, up, uo), down, upward, _ = axes[p]
        tile = HALF // 3
        for t in range(3):
            cols = pl.ds(p * HALF + t * tile, tile)
            w_out = split(wo[:, :, cols].reshape(256, tile))
            part[:, :, :, :, cols] = dot3(rows, w_out).reshape(4, 4, 2, 8, tile)
        for i in range(4):
            relays[p, i] = (
                send(rows_of(p, uo, i, 0), relay.at[p, 0, i], upward),
                send(rows_of(p, uo, i, 1), relay.at[p, 1, i], down),
            )
        for i in range(4):
            direct[p, i] = (
                send(rows_of(p, up, i, 1), sums.at[p, 0, i, 1], upward),
                send(rows_of(p, um, i, 0), sums.at[p, 1, i, 0], down),
            )

    def pass_on(p, i):
        (um, u0, up, uo), down, upward, _ = axes[p]
        relays[p, i][0].wait_recv()
        rows_of(p, up, i, 0)[...] += relay[p, 0, i]
        one = send(rows_of(p, up, i, 0), sums.at[p, 0, i, 0], upward)
        relays[p, i][1].wait_recv()
        rows_of(p, um, i, 1)[...] += relay[p, 1, i]
        second[p, i] = (one, send(rows_of(p, um, i, 1), sums.at[p, 1, i, 1], down))

    def finish(p, i):
        u0 = axes[p][0][1]
        _, down, upward, opposite = axes[1 - p]
        for copy in (*direct[p, i], *second[p, i]):
            copy.wait_recv()
        for h in range(2):
            red[p, i, h] = rows_of(p, u0, i, h)[...] + (sums[p, 0, i, h] + sums[p, 1, i, h])
        if i < 3:
            device = (opposite, down, upward)[i]
            final2[p, i] = send(red.at[p, i], sums2.at[p, i], device)

    for stage in range(6):
        for p in range(2):
            if stage < 4:
                pass_on(p, stage)
            if stage >= 2:
                finish(p, stage - 2)

    ln_copy.wait_recv()
    from_lane = lax.broadcasted_iota(jnp.int32, (256, 512), 0)
    to_lane = lax.broadcasted_iota(jnp.int32, (256, 512), 1)
    to_own = lax.div(from_lane, 16) * 32 + lax.rem(from_lane, 16)
    placed = jnp.zeros((8, 512), f32)
    for value, side in ((ln[core], core), (ln_far[...], 1 - core)):
        place = jnp.where(to_lane == to_own + side * 16, 1.0, 0.0).astype(bf16)
        high, rest = value.astype(bf16), value
        rest = rest - high.astype(f32)
        middle = rest.astype(bf16)
        lowest = (rest - middle.astype(f32)).astype(bf16)
        placed = placed + ((dot(high, place) + dot(middle, place)) + dot(lowest, place))
    ln_out[...] = placed[:1]

    for p in range(2):
        for i in range(3):
            final2[p, i].wait_recv()
        total = red[p, 3] + sums2[p, 0] + (sums2[p, 1] + sums2[p, 2])
        out[:, :, pl.ds(p * HALF, HALF)] = total
    for copy in copies:
        copy.wait_send()


def body(hidden_rows, segment_ids, w_query, w_down, w_up, w_out):
    any_space = pl.BlockSpec(memory_space=pl.ANY)
    vmem = pl.BlockSpec(memory_space=pltpu.VMEM)
    out, ln = pl.pallas_call(
        kernel,
        out_shape=(
            jax.ShapeDtypeStruct((2, 8, D), f32),
            jax.ShapeDtypeStruct((1, TOK_CTX), f32),
        ),
        in_specs=[any_space, vmem, any_space, any_space, any_space, any_space],
        out_specs=(vmem, vmem),
        scratch_shapes=[
            pltpu.VMEM((4, 4, 2, 8, D), f32),
            pltpu.VMEM((4, 4, 2, 2, 9, 8, 128), f32),
            pltpu.VMEM((2, QK, D), f32),
            pltpu.VMEM((KV_RANK + ROPE, D), f32),
            pltpu.VMEM((2, KV_RANK, 256), f32),
            pltpu.VMEM((2, VDIM, D), f32),
            pltpu.VMEM((4, 256, LAT), f32),
            pltpu.VMEM((4, 256, LAT), f32),
            pltpu.VMEM((2, 256, QK), bf16),
            pltpu.VMEM((2, 256, QK), bf16),
            pltpu.VMEM((2, 256, QK), f32),
            pltpu.VMEM((2, 1, 256), f32),
            pltpu.VMEM((2, 1, 256), f32),
            pltpu.VMEM((2, VDIM, 256), f32),
            pltpu.VMEM((4, 4, 2, 8, D), f32),
            pltpu.VMEM((2, 2, 4, 8, HALF), f32),
            pltpu.VMEM((2, 2, 4, 2, 8, HALF), f32),
            pltpu.VMEM((2, 3, 2, 8, HALF), f32),
            pltpu.VMEM((2, 4, 2, 8, HALF), f32),
            pltpu.VMEM((2, 8, 256), f32),
            pltpu.VMEM((8, 256), f32),
            pltpu.SemaphoreType.DMA((N_SEM,)),
            pltpu.SemaphoreType.DMA((N_SEM,)),
            pltpu.SemaphoreType.DMA((8,)),
        ],
        compiler_params=pltpu.CompilerParams(
            collective_id=0, has_side_effects=True, vmem_limit_bytes=58 * 1024 * 1024
        ),
        name="latent_attention",
    )(
        hidden_rows.reshape(2, 8, D), segment_ids.reshape(16, 128),
        w_query.T, w_down.T, w_up, w_out,
    )
    return out.reshape(16, D), ln


def solution(mesh):
    in_specs = (
        P(("ctx", "head"), None),
        P(),
        P(None, "head"),
        P(),
        P(None, "head"),
        P("head", None),
    )
    out_specs = (P(("ctx", "head"), None), P("head", "ctx"))
    return jax.shard_map(body, mesh=mesh, in_specs=in_specs, out_specs=out_specs, check_vma=False)
```

```python
import functools
import math

import jax
import jax.numpy as jnp
from jax import lax
from jax.experimental import pallas as pl
from jax.experimental.pallas import tpu as pltpu
from jax.sharding import PartitionSpec as P

D = 2304
KV_RANK = 512
NOPE = 128
ROPE = 64
VDIM = 128
QK = NOPE + ROPE
TOK_CTX = 512
LAT = 640
HALF = D // 2

eps_norm = 1e-06
neg_fill = -1e30
f32 = jnp.float32
bf16 = jnp.bfloat16
MESH = pl.DeviceIdType.MESH
N_SEM = 200


def split(value):
    high = value.astype(bf16)
    return high, (value - high.astype(f32)).astype(bf16)


def dot(left, right, dims=((1,), (0,))):
    return lax.dot_general(left, right, (dims, ((), ())), preferred_element_type=f32)


def dot3(left, right, dims=((1,), (0,))):
    (left_high, left_low), (right_high, right_low) = left, right
    small = dot(left_high, right_low, dims) + dot(left_low, right_high, dims)
    return dot(left_high, right_high, dims) + small


def kernel(
    x_in, seg_in, wq_in, wd_in, wu_in, wo_in,
    out, ln_out,
    xs, lat, wq, wd, wu, wo, wqh, wql, wuh, wul, woh, wol, kv, kv_far, qh, ql, accq,
    top, tot, acc, part, relay, sums, sums2, red, ln, ln_far,
    send_sem, recv_sem, load_sem,
):
    ctx = lax.axis_index("ctx")
    head = lax.axis_index("head")
    core = lax.rem(head, 2)
    z0 = lax.rem(lax.div(head, 2), 4)
    y0 = lax.div(head, 8)

    def at(y, z):
        return (ctx, (y * 4 + z) * 2 + core)

    def turn(i, by):
        return lax.rem(i + by + 4, 4)

    ym, yp, yo = turn(y0, -1), turn(y0, 1), turn(y0, 2)
    zm, zp, zo = turn(z0, -1), turn(z0, 1), turn(z0, 2)
    Y_UP, Y_DOWN = at(yp, z0), at(ym, z0)
    Z_UP, Z_DOWN = at(y0, zp), at(y0, zm)
    Y_OPP, Z_OPP = at(yo, z0), at(y0, zo)
    PARTNER = (ctx, head + 1 - 2 * core)
    X_UP, X_DOWN, X_OPP = [(turn(ctx, by), head) for by in (1, -1, 2)]

    barrier = pltpu.get_barrier_semaphore()
    peers = [Y_UP, Y_DOWN, Z_UP, Z_DOWN, Y_OPP, Z_OPP, PARTNER, X_UP, X_DOWN, X_OPP]
    for peer in peers:
        pl.semaphore_signal(barrier, inc=1, device_id=peer, device_id_type=MESH)

    loads = []

    def load(src, dst):
        copy = pltpu.make_async_copy(src, dst, load_sem.at[len(loads)])
        copy.start()
        loads.append(copy)
        return copy

    load_x = load(x_in, xs.at[y0, z0])
    WD_STEPS = 3
    wd_rows = D // WD_STEPS
    load_wd = [
        load(wd_in.at[:, pl.ds(i * wd_rows, wd_rows)], wd.at[:, pl.ds(i * wd_rows, wd_rows)])
        for i in range(WD_STEPS)
    ]
    load_rest = [
        load(wq_in, wq.at[core]), load(wu_in, wu.at[core]), load(wo_in, wo.at[core])
    ]
    copies = []

    def send(src, dst, device):
        k = len(copies)
        copy = pltpu.make_async_remote_copy(
            src_ref=src, dst_ref=dst, send_sem=send_sem.at[k], recv_sem=recv_sem.at[k],
            device_id=device, device_id_type=MESH,
        )
        copy.start()
        copies.append(copy)
        return copy

    def gather(view, own=None):
        def hand(y, z, p, h, device):
            return send(view(y, z, p, h), view(y, z, p, h), device)

        first = view(y0, z0, None, None) if own is None else own
        near = [
            send(first, view(y0, z0, None, None), device)
            for device in (Y_UP, Z_UP, Y_DOWN, Z_DOWN, Y_OPP, Z_OPP)
        ]
        yield
        a, b = [], []
        for k, i, j in ((0, ym, zm), (2, yp, zp)):
            near[k].wait_recv()
            a += [hand(i, z0, 0, None, Z_UP), hand(i, z0, 0, None, Z_DOWN)]
            near[k + 1].wait_recv()
            b += [hand(y0, j, 1, None, Y_UP), hand(y0, j, 1, None, Y_DOWN)]
        yield
        near[4].wait_recv()
        a += [hand(yo, z0, 0, None, Z_UP), hand(yo, z0, 0, None, Z_DOWN)]
        near[5].wait_recv()
        b += [hand(y0, zo, 1, None, Y_UP), hand(y0, zo, 1, None, Y_DOWN)]
        yield
        last = []
        for i, (y, z) in enumerate(((ym, zm), (yp, zp), (yo, zo))):
            a[2 * i].wait_recv()
            last.append(hand(y, zm, 0, 0, Z_UP))
            b[2 * i].wait_recv()
            last.append(hand(ym, z, 1, 0, Y_UP))
            a[2 * i + 1].wait_recv()
            last.append(hand(y, zp, 0, 1, Z_DOWN))
            b[2 * i + 1].wait_recv()
            last.append(hand(yp, z, 1, 1, Y_DOWN))
        yield
        for copy in last:
            copy.wait_recv()
        yield

    everything = slice(None)

    def x_view(y, z, p, h):
        cols = everything if p is None else pl.ds(p * HALF, HALF)
        return xs.at[y, z, :, :, cols] if h is None else xs.at[y, z, h, :, cols]

    def gather_small(slot, neighbours=False):
        def whole(y, z):
            return lat.at[y, z, slot]

        def some(y, z, p):
            return lat.at[y, z, slot, (pl.ds(0, 4), pl.ds(4, 5))[p]]

        passed = {}

        def pass_on(y, z, name):
            if neighbours:
                passed[name] = (
                    send(whole(y, z), lat.at[y, z, 2], X_UP),
                    send(whole(y, z), lat.at[y, z, 3], X_DOWN),
                )

        to_y, to_z = (Y_UP, Y_DOWN, Y_OPP), (Z_UP, Z_DOWN, Z_OPP)
        from_y, from_z = (ym, yp, yo), (zm, zp, zo)
        on_y, on_z = [], []
        for k in range(3):
            on_y.append(send(whole(y0, z0), whole(y0, z0), to_y[k]))
            on_z.append(send(whole(y0, z0), whole(y0, z0), to_z[k]))
        pass_on(y0, z0, "own")
        yield passed
        a, b = {}, {}
        for k in range(3):
            on_y[k].wait_recv()
            for j in range(3):
                a[k, j] = send(some(from_y[k], z0, 0), some(from_y[k], z0, 0), to_z[j])
            on_z[k].wait_recv()
            for j in range(3):
                b[j, k] = send(some(y0, from_z[k], 1), some(y0, from_z[k], 1), to_y[j])
            pass_on(from_y[k], z0, ("y", k))
            pass_on(y0, from_z[k], ("z", k))
        yield passed
        for j in range(3):
            for k in range(3):
                a[k, j].wait_recv()
                b[k, j].wait_recv()
                pass_on(from_y[k], from_z[j], (k, j))
        yield passed

    gather_x = gather(x_view, x_in)

    load_x.wait()
    own_high, own_low = split(xs[y0, z0].reshape(16, D))
    own_both = jnp.concatenate([own_high, own_low], axis=0)
    raw2 = jnp.zeros((32, KV_RANK + ROPE), f32)
    raw1 = jnp.zeros((16, KV_RANK + ROPE), f32)
    for i in range(WD_STEPS):
        load_wd[i].wait()
        w_high, w_low = split(wd[:, pl.ds(i * wd_rows, wd_rows)])
        cols = slice(i * wd_rows, (i + 1) * wd_rows)
        raw2 = raw2 + dot(own_both[:, cols], w_high, ((1,), (1,)))
        raw1 = raw1 + dot(own_high[:, cols], w_low, ((1,), (1,)))
        if i == 0:
            pl.semaphore_wait(barrier, len(peers))
            next(gather_x)
            weight_copies = [
                send(wq_in, wq.at[core], PARTNER),
                send(wu_in, wu.at[core], PARTNER),
                send(wo_in, wo.at[core], PARTNER),
            ]
    raw = raw2[:16] + (raw2[16:] + raw1)
    squeezed = raw[:, :KV_RANK]
    mean_square = jnp.mean(squeezed * squeezed, axis=1, keepdims=True)
    squeezed = squeezed * lax.rsqrt(mean_square + eps_norm)
    for j in range(4):
        tiles = squeezed[:, j * 128 : (j + 1) * 128].reshape(2, 8, 128)
        lat[y0, z0, 0, pl.ds(2 * j, 2)] = tiles
    lat[y0, z0, 0, 8] = jnp.concatenate([raw[:8, KV_RANK:], raw[8:, KV_RANK:]], axis=1)

    across = send(lat.at[y0, z0, 0], lat.at[y0, z0, 1], X_OPP)
    gather_own = gather_small(0, neighbours=True)
    gather_opp = gather_small(1)
    passed = next(gather_own)
    next(gather_x)
    next(gather_own)
    next(gather_x)
    across.wait_recv()
    next(gather_opp)
    for copy in load_rest:
        copy.wait()
    for copy in weight_copies:
        copy.wait_recv()
    for h in range(2):
        wqh[h], wql[h] = split(wq[h])
        wuh[h], wul[h] = split(wu[h])
    next(gather_own)
    next(gather_x)
    next(gather_opp)
    woh[...], wol[...] = split(wo[...].reshape(2 * VDIM, D))
    next(gather_x)

    accq[...] = jnp.zeros_like(accq)

    @pl.loop(0, D // 256)
    def _(k):
        cols = pl.ds(pl.multiple_of(k * 256, 256), 256)
        rows = split(xs[:, :, :, :, cols].reshape(256, 256))
        for h in range(2):
            accq[h] += dot3(rows, (wqh[h, :, cols], wql[h, :, cols]), ((1,), (1,)))

    for h in range(2):
        qh[h], ql[h] = split(accq[h] * (1.0 / math.sqrt(QK)))

    ones = jnp.sum(seg_in[...], axis=(0, 1), keepdims=True)
    bound = 2048 - ones
    lane = lax.broadcasted_iota(jnp.int32, (1, 256), 1)
    q_pos = ctx * TOK_CTX + lax.div(lane, 16) * 32 + core * 16 + lax.rem(lane, 16)
    q_start = jnp.where(q_pos >= bound, bound, 0)
    row = lax.broadcasted_iota(jnp.int32, (256, 1), 0)
    row_in, row_block = lax.rem(row, 16), lax.div(row, 16)
    slot_ctx = (ctx, turn(ctx, 2), turn(ctx, -1), turn(ctx, 1))

    top[...] = jnp.full_like(top, neg_fill)
    tot[...] = jnp.zeros_like(tot)
    acc[...] = jnp.zeros_like(acc)

    def attend(block, k_pos):
        allowed = (k_pos <= q_pos) & (k_pos >= q_start)
        for h in range(2):
            keys = jnp.concatenate(
                [block[:, h * 256 : h * 256 + NOPE], block[:, 512 : 512 + ROPE]], axis=1
            )
            scores = dot3(split(keys), (qh[h], ql[h]), ((1,), (1,)))
            scores = jnp.where(allowed, scores, neg_fill)
            old = top[h]
            new = jnp.maximum(old, jnp.max(scores, axis=0, keepdims=True))
            weights = jnp.exp(scores - new)
            factor = jnp.exp(old - new)
            top[h] = new
            tot[h] = tot[h] * factor + jnp.sum(weights, axis=0, keepdims=True)
            values = block[:, h * 256 + NOPE : (h + 1) * 256].T
            acc[h] = acc[h] * factor + dot3(split(values), split(weights))

    def make(g, pieces):
        def columns(tiles):
            taken = [
                lat[:, :, slot, tiles] if z is None else lat[:, z, slot, tiles]
                for slot, z in pieces
            ]
            return jnp.concatenate([value.reshape(-1, 128) for value in taken], axis=0)

        both = split(jnp.concatenate([columns(pl.ds(2 * j, 2)) for j in range(4)], axis=1))
        for h in range(2):
            kv[g, :, pl.ds(h * 256, 256)] = dot3(both, (wuh[h], wul[h]))
        shared = columns(8).reshape(16, 8, 128)
        shared = jnp.concatenate([shared[:, :, :64], shared[:, :, 64:]], axis=1).reshape(256, 64)
        kv[g, :, pl.ds(512, 64)] = shared
        kv[g, :, pl.ds(576, 64)] = jnp.zeros((256, 64), f32)
        return send(kv.at[g], kv_far.at[g], PARTNER)

    def chunk(g, pieces):
        copy = make(g, pieces)
        if len(pieces) == 1:
            at_ctx, block = slot_ctx[pieces[0][0]], row_block
        else:
            pick = lax.div(row, 64)
            at_ctx = jnp.where(pick < 2, slot_ctx[2], slot_ctx[3])
            column = jnp.where(lax.rem(pick, 2) == 0, pieces[0][1], pieces[1][1])
            block = lax.rem(row_block, 4) * 4 + column
        k_pos = at_ctx * TOK_CTX + block * 32 + row_in
        attend(kv[g], k_pos + core * 16)
        copy.wait_recv()
        attend(kv_far[g], k_pos + (1 - core) * 16)

    chunk(0, [(0, None)])
    next(gather_opp)
    chunk(1, [(1, None)])
    names = ["own", ("y", 0), ("y", 1), ("y", 2)], [("z", 0), (0, 0), (1, 0), (2, 0)]
    for name in (*names[0], *names[1]):
        for copy in passed[name]:
            copy.wait_recv()
    chunk(2, [(2, z0), (2, zm), (3, z0), (3, zm)])
    for j in (1, 2):
        for name in (("z", j), (0, j), (1, j), (2, j)):
            for copy in passed[name]:
                copy.wait_recv()
    chunk(3, [(2, zp), (2, zo), (3, zp), (3, zo)])

    heads = []
    for h in range(2):
        ln[h] = jnp.broadcast_to(top[h] + jnp.log(tot[h]), (8, 256))
        heads.append(acc[h] / tot[h])
    ln_copy = send(ln.at[1 - core], ln_far, PARTNER)
    rows = split(jnp.concatenate(heads, axis=0).T)

    on_z = ((zm, z0, zp, zo), Z_DOWN, Z_UP, Z_OPP)
    on_y = ((ym, y0, yp, yo), Y_DOWN, Y_UP, Y_OPP)
    axes = (on_z, on_y)

    def order(p):
        vm, v0, vp, vo = axes[1 - p][0]
        return vo, vm, vp, v0

    def rows_of(p, u, i, h):
        cols = pl.ds(p * HALF, HALF)
        v = order(p)[i]
        return part.at[v, u, h, :, cols] if p == 0 else part.at[u, v, h, :, cols]

    relays, direct, second, final2 = {}, {}, {}, {}
    for p in range(2):
        (um, u0, up, uo), down, upward, _ = axes[p]
        tile = HALF // 3
        for t in range(3):
            cols = pl.ds(p * HALF + t * tile, tile)
            part[:, :, :, :, cols] = dot3(rows, (woh[:, cols], wol[:, cols])).reshape(4, 4, 2, 8, tile)
        for i in range(4):
            relays[p, i] = (
                send(rows_of(p, uo, i, 0), relay.at[p, 0, i], upward),
                send(rows_of(p, uo, i, 1), relay.at[p, 1, i], down),
            )
        for i in range(4):
            direct[p, i] = (
                send(rows_of(p, up, i, 1), sums.at[p, 0, i, 1], upward),
                send(rows_of(p, um, i, 0), sums.at[p, 1, i, 0], down),
            )

    def pass_on(p, i):
        (um, u0, up, uo), down, upward, _ = axes[p]
        relays[p, i][0].wait_recv()
        rows_of(p, up, i, 0)[...] += relay[p, 0, i]
        one = send(rows_of(p, up, i, 0), sums.at[p, 0, i, 0], upward)
        relays[p, i][1].wait_recv()
        rows_of(p, um, i, 1)[...] += relay[p, 1, i]
        second[p, i] = (one, send(rows_of(p, um, i, 1), sums.at[p, 1, i, 1], down))

    def finish(p, i):
        u0 = axes[p][0][1]
        _, down, upward, opposite = axes[1 - p]
        for copy in (*direct[p, i], *second[p, i]):
            copy.wait_recv()
        for h in range(2):
            red[p, i, h] = rows_of(p, u0, i, h)[...] + (sums[p, 0, i, h] + sums[p, 1, i, h])
        if i < 3:
            device = (opposite, down, upward)[i]
            final2[p, i] = send(red.at[p, i], sums2.at[p, i], device)

    for stage in range(6):
        for p in range(2):
            if stage < 4:
                pass_on(p, stage)
            if stage >= 2:
                finish(p, stage - 2)

    ln_copy.wait_recv()
    from_lane = lax.broadcasted_iota(jnp.int32, (256, 512), 0)
    to_lane = lax.broadcasted_iota(jnp.int32, (256, 512), 1)
    to_own = lax.div(from_lane, 16) * 32 + lax.rem(from_lane, 16)
    placed = jnp.zeros((8, 512), f32)
    for value, side in ((ln[core], core), (ln_far[...], 1 - core)):
        place = jnp.where(to_lane == to_own + side * 16, 1.0, 0.0).astype(bf16)
        high, rest = value.astype(bf16), value
        rest = rest - high.astype(f32)
        middle = rest.astype(bf16)
        lowest = (rest - middle.astype(f32)).astype(bf16)
        placed = placed + ((dot(high, place) + dot(middle, place)) + dot(lowest, place))
    ln_out[...] = placed[:1]

    for p in range(2):
        for i in range(3):
            final2[p, i].wait_recv()
        total = red[p, 3] + sums2[p, 0] + (sums2[p, 1] + sums2[p, 2])
        out[:, :, pl.ds(p * HALF, HALF)] = total
    for copy in copies:
        copy.wait_send()


def body(hidden_rows, segment_ids, w_query, w_down, w_up, w_out):
    any_space = pl.BlockSpec(memory_space=pl.ANY)
    vmem = pl.BlockSpec(memory_space=pltpu.VMEM)
    out, ln = pl.pallas_call(
        kernel,
        out_shape=(
            jax.ShapeDtypeStruct((2, 8, D), f32),
            jax.ShapeDtypeStruct((1, TOK_CTX), f32),
        ),
        in_specs=[any_space, vmem, any_space, any_space, any_space, any_space],
        out_specs=(vmem, vmem),
        scratch_shapes=[
            pltpu.VMEM((4, 4, 2, 8, D), f32),
            pltpu.VMEM((4, 4, 4, 9, 8, 128), f32),
            pltpu.VMEM((2, QK, D), f32),
            pltpu.VMEM((KV_RANK + ROPE, D), f32),
            pltpu.VMEM((2, KV_RANK, 256), f32),
            pltpu.VMEM((2, VDIM, D), f32),
            pltpu.VMEM((2, QK, D), bf16),
            pltpu.VMEM((2, QK, D), bf16),
            pltpu.VMEM((2, KV_RANK, 256), bf16),
            pltpu.VMEM((2, KV_RANK, 256), bf16),
            pltpu.VMEM((2 * VDIM, D), bf16),
            pltpu.VMEM((2 * VDIM, D), bf16),
            pltpu.VMEM((4, 256, LAT), f32),
            pltpu.VMEM((4, 256, LAT), f32),
            pltpu.VMEM((2, 256, QK), bf16),
            pltpu.VMEM((2, 256, QK), bf16),
            pltpu.VMEM((2, 256, QK), f32),
            pltpu.VMEM((2, 1, 256), f32),
            pltpu.VMEM((2, 1, 256), f32),
            pltpu.VMEM((2, VDIM, 256), f32),
            pltpu.VMEM((4, 4, 2, 8, D), f32),
            pltpu.VMEM((2, 2, 4, 8, HALF), f32),
            pltpu.VMEM((2, 2, 4, 2, 8, HALF), f32),
            pltpu.VMEM((2, 3, 2, 8, HALF), f32),
            pltpu.VMEM((2, 4, 2, 8, HALF), f32),
            pltpu.VMEM((2, 8, 256), f32),
            pltpu.VMEM((8, 256), f32),
            pltpu.SemaphoreType.DMA((N_SEM,)),
            pltpu.SemaphoreType.DMA((N_SEM,)),
            pltpu.SemaphoreType.DMA((8,)),
        ],
        compiler_params=pltpu.CompilerParams(
            collective_id=0, has_side_effects=True, vmem_limit_bytes=58 * 1024 * 1024
        ),
        name="latent_attention",
    )(
        hidden_rows.reshape(2, 8, D), segment_ids.reshape(16, 128),
        w_query.T, w_down.T, w_up, w_out,
    )
    return out.reshape(16, D), ln


def solution(mesh):
    in_specs = (
        P(("ctx", "head"), None),
        P(),
        P(None, "head"),
        P(),
        P(None, "head"),
        P("head", None),
    )
    out_specs = (P(("ctx", "head"), None), P("head", "ctx"))
    return jax.shard_map(body, mesh=mesh, in_specs=in_specs, out_specs=out_specs, check_vma=False)
```

```python
import functools
import math

import jax
import jax.numpy as jnp
from jax import lax
from jax.experimental import pallas as pl
from jax.experimental.pallas import tpu as pltpu
from jax.sharding import PartitionSpec as P

D = 2304
KV_RANK = 512
NOPE = 128
ROPE = 64
VDIM = 128
QK = NOPE + ROPE
TOK_CTX = 512
LAT = 640
HALF = D // 2

eps_norm = 1e-06
neg_fill = -1e30
f32 = jnp.float32
bf16 = jnp.bfloat16
MESH = pl.DeviceIdType.MESH
N_SEM = 200


def split(value):
    high = value.astype(bf16)
    return high, (value - high.astype(f32)).astype(bf16)


def dot(left, right, dims=((1,), (0,))):
    return lax.dot_general(left, right, (dims, ((), ())), preferred_element_type=f32)


def dot3(left, right, dims=((1,), (0,))):
    (left_high, left_low), (right_high, right_low) = left, right
    small = dot(left_high, right_low, dims) + dot(left_low, right_high, dims)
    return dot(left_high, right_high, dims) + small


def kernel(
    x_in, seg_in, wq_in, wd_in, wu_in, wo_in,
    out, ln_out,
    xs, lat, wq, wd, wu, wo, wqh, wql, wuh, wul, woh, wol, kv, kv_far, qh, ql, accq,
    top, tot, acc, part, relay, sums, sums2, red, ln, ln_far, seg, ln_row, rows_out,
    send_sem, recv_sem, load_sem,
):
    ctx = lax.axis_index("ctx")
    head = lax.axis_index("head")
    core = lax.rem(head, 2)
    z0 = lax.rem(lax.div(head, 2), 4)
    y0 = lax.div(head, 8)

    def at(y, z):
        return (ctx, (y * 4 + z) * 2 + core)

    def turn(i, by):
        return lax.rem(i + by + 4, 4)

    ym, yp, yo = turn(y0, -1), turn(y0, 1), turn(y0, 2)
    zm, zp, zo = turn(z0, -1), turn(z0, 1), turn(z0, 2)
    Y_UP, Y_DOWN = at(yp, z0), at(ym, z0)
    Z_UP, Z_DOWN = at(y0, zp), at(y0, zm)
    Y_OPP, Z_OPP = at(yo, z0), at(y0, zo)
    PARTNER = (ctx, head + 1 - 2 * core)
    X_UP, X_DOWN, X_OPP = [(turn(ctx, by), head) for by in (1, -1, 2)]

    barrier = pltpu.get_barrier_semaphore()
    peers = [Y_UP, Y_DOWN, Z_UP, Z_DOWN, Y_OPP, Z_OPP, PARTNER, X_UP, X_DOWN, X_OPP]
    for peer in peers:
        pl.semaphore_signal(barrier, inc=1, device_id=peer, device_id_type=MESH)

    loads = []

    def load(src, dst):
        copy = pltpu.make_async_copy(src, dst, load_sem.at[len(loads)])
        copy.start()
        loads.append(copy)
        return copy

    load_x = load(x_in, xs.at[y0, z0])
    WD_STEPS = 3
    wd_rows = D // WD_STEPS
    load_wd = [
        load(wd_in.at[:, pl.ds(i * wd_rows, wd_rows)], wd.at[:, pl.ds(i * wd_rows, wd_rows)])
        for i in range(WD_STEPS)
    ]
    load_rest = [
        load(wq_in, wq.at[core]), load(wu_in, wu.at[core]), load(wo_in, wo.at[core]),
        load(seg_in, seg),
    ]
    copies = []

    def send(src, dst, device):
        k = len(copies)
        copy = pltpu.make_async_remote_copy(
            src_ref=src, dst_ref=dst, send_sem=send_sem.at[k], recv_sem=recv_sem.at[k],
            device_id=device, device_id_type=MESH,
        )
        copy.start()
        copies.append(copy)
        return copy

    def gather(view, own=None):
        def hand(y, z, p, h, device):
            return send(view(y, z, p, h), view(y, z, p, h), device)

        first = view(y0, z0, None, None) if own is None else own
        near = [
            send(first, view(y0, z0, None, None), device)
            for device in (Y_UP, Z_UP, Y_DOWN, Z_DOWN, Y_OPP, Z_OPP)
        ]
        yield
        a, b = [], []
        for k, i, j in ((0, ym, zm), (2, yp, zp)):
            near[k].wait_recv()
            a += [hand(i, z0, 0, None, Z_UP), hand(i, z0, 0, None, Z_DOWN)]
            near[k + 1].wait_recv()
            b += [hand(y0, j, 1, None, Y_UP), hand(y0, j, 1, None, Y_DOWN)]
        yield
        near[4].wait_recv()
        a += [hand(yo, z0, 0, None, Z_UP), hand(yo, z0, 0, None, Z_DOWN)]
        near[5].wait_recv()
        b += [hand(y0, zo, 1, None, Y_UP), hand(y0, zo, 1, None, Y_DOWN)]
        yield
        last = []
        for i, (y, z) in enumerate(((ym, zm), (yp, zp), (yo, zo))):
            a[2 * i].wait_recv()
            last.append(hand(y, zm, 0, 0, Z_UP))
            b[2 * i].wait_recv()
            last.append(hand(ym, z, 1, 0, Y_UP))
            a[2 * i + 1].wait_recv()
            last.append(hand(y, zp, 0, 1, Z_DOWN))
            b[2 * i + 1].wait_recv()
            last.append(hand(yp, z, 1, 1, Y_DOWN))
        yield
        for copy in last:
            copy.wait_recv()
        yield

    everything = slice(None)

    def x_view(y, z, p, h):
        cols = everything if p is None else pl.ds(p * HALF, HALF)
        return xs.at[y, z, :, :, cols] if h is None else xs.at[y, z, h, :, cols]

    def gather_small(slot, neighbours=False):
        def whole(y, z):
            return lat.at[y, z, slot]

        def some(y, z, p):
            return lat.at[y, z, slot, (pl.ds(0, 4), pl.ds(4, 5))[p]]

        passed = {}

        def pass_on(y, z, name):
            if neighbours:
                passed[name] = (
                    send(whole(y, z), lat.at[y, z, 2], X_UP),
                    send(whole(y, z), lat.at[y, z, 3], X_DOWN),
                )

        to_y, to_z = (Y_UP, Y_DOWN, Y_OPP), (Z_UP, Z_DOWN, Z_OPP)
        from_y, from_z = (ym, yp, yo), (zm, zp, zo)
        on_y, on_z = [], []
        for k in range(3):
            on_y.append(send(whole(y0, z0), whole(y0, z0), to_y[k]))
            on_z.append(send(whole(y0, z0), whole(y0, z0), to_z[k]))
        pass_on(y0, z0, "own")
        yield passed
        a, b = {}, {}
        for k in range(3):
            on_y[k].wait_recv()
            for j in range(3):
                a[k, j] = send(some(from_y[k], z0, 0), some(from_y[k], z0, 0), to_z[j])
            on_z[k].wait_recv()
            for j in range(3):
                b[j, k] = send(some(y0, from_z[k], 1), some(y0, from_z[k], 1), to_y[j])
            pass_on(from_y[k], z0, ("y", k))
            pass_on(y0, from_z[k], ("z", k))
        yield passed
        for j in range(3):
            for k in range(3):
                a[k, j].wait_recv()
                b[k, j].wait_recv()
                pass_on(from_y[k], from_z[j], (k, j))
        yield passed

    def make(g, pieces):
        def columns(tiles):
            taken = [
                lat[:, :, slot, tiles] if z is None else lat[:, z, slot, tiles]
                for slot, z in pieces
            ]
            return jnp.concatenate([value.reshape(-1, 128) for value in taken], axis=0)

        both = split(jnp.concatenate([columns(pl.ds(2 * j, 2)) for j in range(4)], axis=1))
        for h in range(2):
            kv[g, :, pl.ds(h * 256, 256)] = dot3(both, (wuh[h], wul[h]))
        shared = columns(8).reshape(16, 8, 128)
        shared = jnp.concatenate([shared[:, :, :64], shared[:, :, 64:]], axis=1).reshape(256, 64)
        kv[g, :, pl.ds(512, 64)] = shared
        kv[g, :, pl.ds(576, 64)] = jnp.zeros((256, 64), f32)
        return send(kv.at[g], kv_far.at[g], PARTNER)

    gather_x = gather(x_view, x_in)

    load_x.wait()
    own_high, own_low = split(xs[y0, z0].reshape(16, D))
    own_both = jnp.concatenate([own_high, own_low], axis=0)
    raw2 = jnp.zeros((32, KV_RANK + ROPE), f32)
    raw1 = jnp.zeros((16, KV_RANK + ROPE), f32)
    for i in range(WD_STEPS):
        load_wd[i].wait()
        w_high, w_low = split(wd[:, pl.ds(i * wd_rows, wd_rows)])
        cols = slice(i * wd_rows, (i + 1) * wd_rows)
        raw2 = raw2 + dot(own_both[:, cols], w_high, ((1,), (1,)))
        raw1 = raw1 + dot(own_high[:, cols], w_low, ((1,), (1,)))
        if i == 0:
            pl.semaphore_wait(barrier, len(peers))
            next(gather_x)
            weight_copies = [
                send(wq_in, wq.at[core], PARTNER),
                send(wu_in, wu.at[core], PARTNER),
                send(wo_in, wo.at[core], PARTNER),
            ]
    raw = raw2[:16] + (raw2[16:] + raw1)
    squeezed = raw[:, :KV_RANK]
    mean_square = jnp.mean(squeezed * squeezed, axis=1, keepdims=True)
    squeezed = squeezed * lax.rsqrt(mean_square + eps_norm)
    for j in range(4):
        tiles = squeezed[:, j * 128 : (j + 1) * 128].reshape(2, 8, 128)
        lat[y0, z0, 0, pl.ds(2 * j, 2)] = tiles
    lat[y0, z0, 0, 8] = jnp.concatenate([raw[:8, KV_RANK:], raw[8:, KV_RANK:]], axis=1)

    across = send(lat.at[y0, z0, 0], lat.at[y0, z0, 1], X_OPP)
    gather_own = gather_small(0, neighbours=True)
    gather_opp = gather_small(1)
    passed = next(gather_own)
    for copy in load_rest:
        copy.wait()
    for copy in weight_copies:
        copy.wait_recv()
    for h in range(2):
        wqh[h], wql[h] = split(wq[h])
    next(gather_x)
    next(gather_x)
    next(gather_own)
    next(gather_x)
    for h in range(2):
        wuh[h], wul[h] = split(wu[h])
    across.wait_recv()
    next(gather_opp)
    next(gather_own)
    made = {0: make(0, [(0, None)])}
    next(gather_opp)
    woh[...], wol[...] = split(wo[...].reshape(2 * VDIM, D))
    next(gather_x)

    accq[...] = jnp.zeros_like(accq)

    @pl.loop(0, D // 256)
    def _(k):
        cols = pl.ds(pl.multiple_of(k * 256, 256), 256)
        rows = split(xs[:, :, :, :, cols].reshape(256, 256))
        for h in range(2):
            accq[h] += dot3(rows, (wqh[h, :, cols], wql[h, :, cols]), ((1,), (1,)))

    for h in range(2):
        qh[h], ql[h] = split(accq[h] * (1.0 / math.sqrt(QK)))

    ones = jnp.sum(seg[...], axis=(0, 1), keepdims=True)
    bound = 2048 - ones
    lane = lax.broadcasted_iota(jnp.int32, (1, 256), 1)
    q_pos = ctx * TOK_CTX + lax.div(lane, 16) * 32 + core * 16 + lax.rem(lane, 16)
    q_start = jnp.where(q_pos >= bound, bound, 0)
    row = lax.broadcasted_iota(jnp.int32, (256, 1), 0)
    row_in, row_block = lax.rem(row, 16), lax.div(row, 16)
    slot_ctx = (ctx, turn(ctx, 2), turn(ctx, -1), turn(ctx, 1))

    top[...] = jnp.full_like(top, neg_fill)
    tot[...] = jnp.zeros_like(tot)
    acc[...] = jnp.zeros_like(acc)

    def attend(block, k_pos):
        allowed = (k_pos <= q_pos) & (k_pos >= q_start)
        for h in range(2):
            keys = jnp.concatenate(
                [block[:, h * 256 : h * 256 + NOPE], block[:, 512 : 512 + ROPE]], axis=1
            )
            scores = dot3(split(keys), (qh[h], ql[h]), ((1,), (1,)))
            scores = jnp.where(allowed, scores, neg_fill)
            old = top[h]
            new = jnp.maximum(old, jnp.max(scores, axis=0, keepdims=True))
            weights = jnp.exp(scores - new)
            factor = jnp.exp(old - new)
            top[h] = new
            tot[h] = tot[h] * factor + jnp.sum(weights, axis=0, keepdims=True)
            values = block[:, h * 256 + NOPE : (h + 1) * 256].T
            acc[h] = acc[h] * factor + dot3(split(values), split(weights))

    def positions(pieces):
        if len(pieces) == 1:
            at_ctx, block = slot_ctx[pieces[0][0]], row_block
        else:
            pick = lax.div(row, 64)
            at_ctx = jnp.where(pick < 2, slot_ctx[2], slot_ctx[3])
            column = jnp.where(lax.rem(pick, 2) == 0, pieces[0][1], pieces[1][1])
            block = lax.rem(row_block, 4) * 4 + column
        return at_ctx * TOK_CTX + block * 32 + row_in

    def arrive(names):
        for name in names:
            for copy in passed[name]:
                copy.wait_recv()

    chunks = (
        [(0, None)],
        [(1, None)],
        [(2, z0), (2, zm), (3, z0), (3, zm)],
        [(2, zp), (2, zo), (3, zp), (3, zo)],
    )
    near = ["own", ("y", 0), ("y", 1), ("y", 2), ("z", 0), (0, 0), (1, 0), (2, 0)]
    far = [(name, j) for j in (1, 2) for name in ("z", 0, 1, 2)]
    attend(kv[0], positions(chunks[0]) + core * 16)
    next(gather_opp)
    made[1] = make(1, chunks[1])
    made[0].wait_recv()
    attend(kv_far[0], positions(chunks[0]) + (1 - core) * 16)
    attend(kv[1], positions(chunks[1]) + core * 16)
    arrive(near)
    made[2] = make(2, chunks[2])
    made[1].wait_recv()
    attend(kv_far[1], positions(chunks[1]) + (1 - core) * 16)
    attend(kv[2], positions(chunks[2]) + core * 16)
    arrive(far)
    made[3] = make(3, chunks[3])
    made[2].wait_recv()
    attend(kv_far[2], positions(chunks[2]) + (1 - core) * 16)
    attend(kv[3], positions(chunks[3]) + core * 16)
    made[3].wait_recv()
    attend(kv_far[3], positions(chunks[3]) + (1 - core) * 16)

    heads = []
    for h in range(2):
        ln[h] = jnp.broadcast_to(top[h] + jnp.log(tot[h]), (8, 256))
        heads.append(acc[h] / tot[h])
    ln_copy = send(ln.at[1 - core], ln_far, PARTNER)
    rows = split(jnp.concatenate(heads, axis=0).T)

    on_z = ((zm, z0, zp, zo), Z_DOWN, Z_UP, Z_OPP)
    on_y = ((ym, y0, yp, yo), Y_DOWN, Y_UP, Y_OPP)
    axes = (on_z, on_y)

    def order(p):
        vm, v0, vp, vo = axes[1 - p][0]
        return vo, vm, vp, v0

    def rows_of(p, u, i, h):
        cols = pl.ds(p * HALF, HALF)
        v = order(p)[i]
        return part.at[v, u, h, :, cols] if p == 0 else part.at[u, v, h, :, cols]

    relays, direct, second, final2 = {}, {}, {}, {}
    for p in range(2):
        (um, u0, up, uo), down, upward, _ = axes[p]
        tile = HALF // 3
        for t in range(3):
            cols = pl.ds(p * HALF + t * tile, tile)
            part[:, :, :, :, cols] = dot3(rows, (woh[:, cols], wol[:, cols])).reshape(4, 4, 2, 8, tile)
        for i in range(4):
            relays[p, i] = (
                send(rows_of(p, uo, i, 0), relay.at[p, 0, i], upward),
                send(rows_of(p, uo, i, 1), relay.at[p, 1, i], down),
            )
        for i in range(4):
            direct[p, i] = (
                send(rows_of(p, up, i, 1), sums.at[p, 0, i, 1], upward),
                send(rows_of(p, um, i, 0), sums.at[p, 1, i, 0], down),
            )

    def pass_on(p, i):
        (um, u0, up, uo), down, upward, _ = axes[p]
        relays[p, i][0].wait_recv()
        rows_of(p, up, i, 0)[...] += relay[p, 0, i]
        one = send(rows_of(p, up, i, 0), sums.at[p, 0, i, 0], upward)
        relays[p, i][1].wait_recv()
        rows_of(p, um, i, 1)[...] += relay[p, 1, i]
        second[p, i] = (one, send(rows_of(p, um, i, 1), sums.at[p, 1, i, 1], down))

    def finish(p, i):
        u0 = axes[p][0][1]
        _, down, upward, opposite = axes[1 - p]
        for copy in (*direct[p, i], *second[p, i]):
            copy.wait_recv()
        for h in range(2):
            red[p, i, h] = rows_of(p, u0, i, h)[...] + (sums[p, 0, i, h] + sums[p, 1, i, h])
        if i < 3:
            device = (opposite, down, upward)[i]
            final2[p, i] = send(red.at[p, i], sums2.at[p, i], device)

    for stage in range(6):
        for p in range(2):
            if stage < 4:
                pass_on(p, stage)
            if stage >= 2:
                finish(p, stage - 2)

    ln_copy.wait_recv()
    from_lane = lax.broadcasted_iota(jnp.int32, (256, 512), 0)
    to_lane = lax.broadcasted_iota(jnp.int32, (256, 512), 1)
    to_own = lax.div(from_lane, 16) * 32 + lax.rem(from_lane, 16)
    placed = jnp.zeros((8, 512), f32)
    for value, side in ((ln[core], core), (ln_far[...], 1 - core)):
        place = jnp.where(to_lane == to_own + side * 16, 1.0, 0.0).astype(bf16)
        high, rest = value.astype(bf16), value
        rest = rest - high.astype(f32)
        middle = rest.astype(bf16)
        lowest = (rest - middle.astype(f32)).astype(bf16)
        placed = placed + ((dot(high, place) + dot(middle, place)) + dot(lowest, place))
    ln_row[...] = placed[:1]
    stores = [load(ln_row, ln_out)]

    for p in range(2):
        for i in range(3):
            final2[p, i].wait_recv()
        total = red[p, 3] + sums2[p, 0] + (sums2[p, 1] + sums2[p, 2])
        rows_out[:, :, pl.ds(p * HALF, HALF)] = total
        cols = pl.ds(p * HALF, HALF)
        stores.append(load(rows_out.at[:, :, cols], out.at[:, :, cols]))
    for copy in stores:
        copy.wait()
    for copy in copies:
        copy.wait_send()


def body(hidden_rows, segment_ids, w_query, w_down, w_up, w_out):
    any_space = pl.BlockSpec(memory_space=pl.ANY)
    out, ln = pl.pallas_call(
        kernel,
        out_shape=(
            jax.ShapeDtypeStruct((2, 8, D), f32),
            jax.ShapeDtypeStruct((1, TOK_CTX), f32),
        ),
        in_specs=[any_space] * 6,
        out_specs=(any_space, any_space),
        scratch_shapes=[
            pltpu.VMEM((4, 4, 2, 8, D), f32),
            pltpu.VMEM((4, 4, 4, 9, 8, 128), f32),
            pltpu.VMEM((2, QK, D), f32),
            pltpu.VMEM((KV_RANK + ROPE, D), f32),
            pltpu.VMEM((2, KV_RANK, 256), f32),
            pltpu.VMEM((2, VDIM, D), f32),
            pltpu.VMEM((2, QK, D), bf16),
            pltpu.VMEM((2, QK, D), bf16),
            pltpu.VMEM((2, KV_RANK, 256), bf16),
            pltpu.VMEM((2, KV_RANK, 256), bf16),
            pltpu.VMEM((2 * VDIM, D), bf16),
            pltpu.VMEM((2 * VDIM, D), bf16),
            pltpu.VMEM((4, 256, LAT), f32),
            pltpu.VMEM((4, 256, LAT), f32),
            pltpu.VMEM((2, 256, QK), bf16),
            pltpu.VMEM((2, 256, QK), bf16),
            pltpu.VMEM((2, 256, QK), f32),
            pltpu.VMEM((2, 1, 256), f32),
            pltpu.VMEM((2, 1, 256), f32),
            pltpu.VMEM((2, VDIM, 256), f32),
            pltpu.VMEM((4, 4, 2, 8, D), f32),
            pltpu.VMEM((2, 2, 4, 8, HALF), f32),
            pltpu.VMEM((2, 2, 4, 2, 8, HALF), f32),
            pltpu.VMEM((2, 3, 2, 8, HALF), f32),
            pltpu.VMEM((2, 4, 2, 8, HALF), f32),
            pltpu.VMEM((2, 8, 256), f32),
            pltpu.VMEM((8, 256), f32),
            pltpu.VMEM((16, 128), jnp.int32),
            pltpu.VMEM((1, TOK_CTX), f32),
            pltpu.VMEM((2, 8, D), f32),
            pltpu.SemaphoreType.DMA((N_SEM,)),
            pltpu.SemaphoreType.DMA((N_SEM,)),
            pltpu.SemaphoreType.DMA((16,)),
        ],
        compiler_params=pltpu.CompilerParams(
            collective_id=0, has_side_effects=True, vmem_limit_bytes=58 * 1024 * 1024
        ),
        name="latent_attention",
    )(
        hidden_rows.reshape(2, 8, D), segment_ids.reshape(16, 128),
        w_query.T, w_down.T, w_up, w_out,
    )
    return out.reshape(16, D), ln


def solution(mesh):
    in_specs = (
        P(("ctx", "head"), None),
        P(),
        P(None, "head"),
        P(),
        P(None, "head"),
        P("head", None),
    )
    out_specs = (P(("ctx", "head"), None), P("head", "ctx"))
    return jax.shard_map(body, mesh=mesh, in_specs=in_specs, out_specs=out_specs, check_vma=False)
```

```python
import functools
import math

import jax
import jax.numpy as jnp
from jax import lax
from jax.experimental import pallas as pl
from jax.experimental.pallas import tpu as pltpu
from jax.sharding import PartitionSpec as P

D = 2304
KV_RANK = 512
NOPE = 128
ROPE = 64
VDIM = 128
QK = NOPE + ROPE
TOK_CTX = 512
LAT = 640
HALF = D // 2

eps_norm = 1e-06
neg_fill = -1e30
f32 = jnp.float32
bf16 = jnp.bfloat16
MESH = pl.DeviceIdType.MESH
N_SEM = 200


def split(value):
    high = value.astype(bf16)
    return high, (value - high.astype(f32)).astype(bf16)


def dot(left, right, dims=((1,), (0,))):
    return lax.dot_general(left, right, (dims, ((), ())), preferred_element_type=f32)


def dot3(left, right, dims=((1,), (0,))):
    (left_high, left_low), (right_high, right_low) = left, right
    small = dot(left_high, right_low, dims) + dot(left_low, right_high, dims)
    return dot(left_high, right_high, dims) + small


def kernel(
    x_in, seg_in, wq_in, wd_in, wu_in, wo_in,
    out, ln_out,
    xs, lat, wq, wd, wu, wo, wqh, wql, wuh, wul, woh, wol, kv, kv_far, qh, ql, accq,
    top, tot, acc, part, relay, sums, sums2, red, ln, ln_far, seg, ln_row, rows_out, xh, xl,
    send_sem, recv_sem, load_sem,
):
    ctx = lax.axis_index("ctx")
    head = lax.axis_index("head")
    core = lax.rem(head, 2)
    z0 = lax.rem(lax.div(head, 2), 4)
    y0 = lax.div(head, 8)

    def at(y, z):
        return (ctx, (y * 4 + z) * 2 + core)

    def turn(i, by):
        return lax.rem(i + by + 4, 4)

    ym, yp, yo = turn(y0, -1), turn(y0, 1), turn(y0, 2)
    zm, zp, zo = turn(z0, -1), turn(z0, 1), turn(z0, 2)
    Y_UP, Y_DOWN = at(yp, z0), at(ym, z0)
    Z_UP, Z_DOWN = at(y0, zp), at(y0, zm)
    Y_OPP, Z_OPP = at(yo, z0), at(y0, zo)
    PARTNER = (ctx, head + 1 - 2 * core)
    X_UP, X_DOWN, X_OPP = [(turn(ctx, by), head) for by in (1, -1, 2)]

    barrier = pltpu.get_barrier_semaphore()
    peers = [Y_UP, Y_DOWN, Z_UP, Z_DOWN, Y_OPP, Z_OPP, PARTNER, X_UP, X_DOWN, X_OPP]
    for peer in peers:
        pl.semaphore_signal(barrier, inc=1, device_id=peer, device_id_type=MESH)

    loads = []

    def load(src, dst):
        copy = pltpu.make_async_copy(src, dst, load_sem.at[len(loads)])
        copy.start()
        loads.append(copy)
        return copy

    load_x = load(x_in, xs.at[y0, z0])
    WD_STEPS = 3
    wd_rows = D // WD_STEPS
    load_wd = [
        load(wd_in.at[:, pl.ds(i * wd_rows, wd_rows)], wd.at[:, pl.ds(i * wd_rows, wd_rows)])
        for i in range(WD_STEPS)
    ]
    load_rest = [
        load(wq_in, wq.at[core]), load(wu_in, wu.at[core]), load(wo_in, wo.at[core]),
        load(seg_in, seg),
    ]
    copies = []

    def send(src, dst, device):
        k = len(copies)
        copy = pltpu.make_async_remote_copy(
            src_ref=src, dst_ref=dst, send_sem=send_sem.at[k], recv_sem=recv_sem.at[k],
            device_id=device, device_id_type=MESH,
        )
        copy.start()
        copies.append(copy)
        return copy

    def gather(view, own=None):
        def hand(y, z, p, h, device):
            return send(view(y, z, p, h), view(y, z, p, h), device)

        first = view(y0, z0, None, None) if own is None else own
        near = [
            send(first, view(y0, z0, None, None), device)
            for device in (Y_UP, Z_UP, Y_DOWN, Z_DOWN, Y_OPP, Z_OPP)
        ]
        yield
        a, b = [], []
        for k, i, j in ((0, ym, zm), (2, yp, zp)):
            near[k].wait_recv()
            a += [hand(i, z0, 0, None, Z_UP), hand(i, z0, 0, None, Z_DOWN)]
            near[k + 1].wait_recv()
            b += [hand(y0, j, 1, None, Y_UP), hand(y0, j, 1, None, Y_DOWN)]
        yield
        near[4].wait_recv()
        a += [hand(yo, z0, 0, None, Z_UP), hand(yo, z0, 0, None, Z_DOWN)]
        near[5].wait_recv()
        b += [hand(y0, zo, 1, None, Y_UP), hand(y0, zo, 1, None, Y_DOWN)]
        yield
        last = []
        for i, (y, z) in enumerate(((ym, zm), (yp, zp), (yo, zo))):
            a[2 * i].wait_recv()
            last.append(hand(y, zm, 0, 0, Z_UP))
            b[2 * i].wait_recv()
            last.append(hand(ym, z, 1, 0, Y_UP))
            a[2 * i + 1].wait_recv()
            last.append(hand(y, zp, 0, 1, Z_DOWN))
            b[2 * i + 1].wait_recv()
            last.append(hand(yp, z, 1, 1, Y_DOWN))
        yield
        for copy in last:
            copy.wait_recv()
        yield

    everything = slice(None)

    def x_view(y, z, p, h):
        cols = everything if p is None else pl.ds(p * HALF, HALF)
        return xs.at[y, z, :, :, cols] if h is None else xs.at[y, z, h, :, cols]

    def gather_small(slot, neighbours=False):
        def whole(y, z):
            return lat.at[y, z, slot]

        def some(y, z, p):
            return lat.at[y, z, slot, (pl.ds(0, 4), pl.ds(4, 5))[p]]

        passed = {}

        def pass_on(y, z, name):
            if neighbours:
                passed[name] = (
                    send(whole(y, z), lat.at[y, z, 2], X_UP),
                    send(whole(y, z), lat.at[y, z, 3], X_DOWN),
                )

        to_y, to_z = (Y_UP, Y_DOWN, Y_OPP), (Z_UP, Z_DOWN, Z_OPP)
        from_y, from_z = (ym, yp, yo), (zm, zp, zo)
        on_y, on_z = [], []
        for k in range(3):
            on_y.append(send(whole(y0, z0), whole(y0, z0), to_y[k]))
            on_z.append(send(whole(y0, z0), whole(y0, z0), to_z[k]))
        pass_on(y0, z0, "own")
        yield passed
        a, b = {}, {}
        for k in range(3):
            on_y[k].wait_recv()
            for j in range(3):
                a[k, j] = send(some(from_y[k], z0, 0), some(from_y[k], z0, 0), to_z[j])
            on_z[k].wait_recv()
            for j in range(3):
                b[j, k] = send(some(y0, from_z[k], 1), some(y0, from_z[k], 1), to_y[j])
            pass_on(from_y[k], z0, ("y", k))
            pass_on(y0, from_z[k], ("z", k))
        yield passed
        for j in range(3):
            for k in range(3):
                a[k, j].wait_recv()
                b[k, j].wait_recv()
                pass_on(from_y[k], from_z[j], (k, j))
        yield passed

    def make(g, pieces):
        def columns(tiles):
            taken = [
                lat[:, :, slot, tiles] if z is None else lat[:, z, slot, tiles]
                for slot, z in pieces
            ]
            return jnp.concatenate([value.reshape(-1, 128) for value in taken], axis=0)

        both = split(jnp.concatenate([columns(pl.ds(2 * j, 2)) for j in range(4)], axis=1))
        for h in range(2):
            kv[g, :, pl.ds(h * 256, 256)] = dot3(both, (wuh[h], wul[h]))
        shared = columns(8).reshape(16, 8, 128)
        shared = jnp.concatenate([shared[:, :, :64], shared[:, :, 64:]], axis=1).reshape(256, 64)
        kv[g, :, pl.ds(512, 64)] = shared
        kv[g, :, pl.ds(576, 64)] = jnp.zeros((256, 64), f32)
        return send(kv.at[g], kv_far.at[g], PARTNER)

    gather_x = gather(x_view, x_in)

    load_x.wait()
    own_high, own_low = split(xs[y0, z0].reshape(16, D))
    own_both = jnp.concatenate([own_high, own_low], axis=0)
    raw2 = jnp.zeros((32, KV_RANK + ROPE), f32)
    raw1 = jnp.zeros((16, KV_RANK + ROPE), f32)
    for i in range(WD_STEPS):
        load_wd[i].wait()
        w_high, w_low = split(wd[:, pl.ds(i * wd_rows, wd_rows)])
        cols = slice(i * wd_rows, (i + 1) * wd_rows)
        raw2 = raw2 + dot(own_both[:, cols], w_high, ((1,), (1,)))
        raw1 = raw1 + dot(own_high[:, cols], w_low, ((1,), (1,)))
        if i == 0:
            pl.semaphore_wait(barrier, len(peers))
            next(gather_x)
            weight_copies = [
                send(wq_in, wq.at[core], PARTNER),
                send(wu_in, wu.at[core], PARTNER),
                send(wo_in, wo.at[core], PARTNER),
            ]
    raw = raw2[:16] + (raw2[16:] + raw1)
    squeezed = raw[:, :KV_RANK]
    mean_square = jnp.mean(squeezed * squeezed, axis=1, keepdims=True)
    squeezed = squeezed * lax.rsqrt(mean_square + eps_norm)
    for j in range(4):
        tiles = squeezed[:, j * 128 : (j + 1) * 128].reshape(2, 8, 128)
        lat[y0, z0, 0, pl.ds(2 * j, 2)] = tiles
    lat[y0, z0, 0, 8] = jnp.concatenate([raw[:8, KV_RANK:], raw[8:, KV_RANK:]], axis=1)

    across = send(lat.at[y0, z0, 0], lat.at[y0, z0, 1], X_OPP)
    gather_own = gather_small(0, neighbours=True)
    gather_opp = gather_small(1)
    passed = next(gather_own)
    for copy in load_rest:
        copy.wait()
    for copy in weight_copies:
        copy.wait_recv()
    for h in range(2):
        wqh[h], wql[h] = split(wq[h])
    next(gather_x)
    next(gather_x)
    next(gather_own)
    next(gather_x)
    for h in range(2):
        wuh[h], wul[h] = split(wu[h])
    across.wait_recv()
    next(gather_opp)
    next(gather_own)
    made = {0: make(0, [(0, None)])}
    next(gather_opp)
    woh[...], wol[...] = split(wo[...].reshape(2 * VDIM, D))
    next(gather_x)

    accq[...] = jnp.zeros_like(accq)
    xh[...], xl[...] = split(xs[...].reshape(256, D))
    for h in range(2):
        accq[h] = dot3((xh[...], xl[...]), (wqh[h], wql[h]), ((1,), (1,)))

    for h in range(2):
        qh[h], ql[h] = split(accq[h] * (1.0 / math.sqrt(QK)))

    ones = jnp.sum(seg[...], axis=(0, 1), keepdims=True)
    bound = 2048 - ones
    lane = lax.broadcasted_iota(jnp.int32, (1, 256), 1)
    q_pos = ctx * TOK_CTX + lax.div(lane, 16) * 32 + core * 16 + lax.rem(lane, 16)
    q_start = jnp.where(q_pos >= bound, bound, 0)
    row = lax.broadcasted_iota(jnp.int32, (256, 1), 0)
    row_in, row_block = lax.rem(row, 16), lax.div(row, 16)
    slot_ctx = (ctx, turn(ctx, 2), turn(ctx, -1), turn(ctx, 1))

    top[...] = jnp.full_like(top, neg_fill)
    tot[...] = jnp.zeros_like(tot)
    acc[...] = jnp.zeros_like(acc)

    def attend(block, k_pos):
        allowed = (k_pos <= q_pos) & (k_pos >= q_start)
        found, stats = [], []
        for h in range(2):
            keys = jnp.concatenate(
                [block[:, h * 256 : h * 256 + NOPE], block[:, 512 : 512 + ROPE]], axis=1
            )
            scores = dot3(split(keys), (qh[h], ql[h]), ((1,), (1,)))
            found.append(jnp.where(allowed, scores, neg_fill))
        for h in range(2):
            old = top[h]
            new = jnp.maximum(old, jnp.max(found[h], axis=0, keepdims=True))
            weights = jnp.exp(found[h] - new)
            factor = jnp.exp(old - new)
            top[h] = new
            tot[h] = tot[h] * factor + jnp.sum(weights, axis=0, keepdims=True)
            stats.append((factor, split(weights)))
        for h in range(2):
            values = split(block[:, h * 256 + NOPE : (h + 1) * 256].T)
            acc[h] = acc[h] * stats[h][0] + dot3(values, stats[h][1])

    def positions(pieces):
        if len(pieces) == 1:
            at_ctx, block = slot_ctx[pieces[0][0]], row_block
        else:
            pick = lax.div(row, 64)
            at_ctx = jnp.where(pick < 2, slot_ctx[2], slot_ctx[3])
            column = jnp.where(lax.rem(pick, 2) == 0, pieces[0][1], pieces[1][1])
            block = lax.rem(row_block, 4) * 4 + column
        return at_ctx * TOK_CTX + block * 32 + row_in

    def arrive(names):
        for name in names:
            for copy in passed[name]:
                copy.wait_recv()

    chunks = (
        [(0, None)],
        [(1, None)],
        [(2, z0), (2, zm), (3, z0), (3, zm)],
        [(2, zp), (2, zo), (3, zp), (3, zo)],
    )
    near = ["own", ("y", 0), ("y", 1), ("y", 2), ("z", 0), (0, 0), (1, 0), (2, 0)]
    far = [(name, j) for j in (1, 2) for name in ("z", 0, 1, 2)]
    attend(kv[0], positions(chunks[0]) + core * 16)
    next(gather_opp)
    made[1] = make(1, chunks[1])
    made[0].wait_recv()
    attend(kv_far[0], positions(chunks[0]) + (1 - core) * 16)
    attend(kv[1], positions(chunks[1]) + core * 16)
    arrive(near)
    made[2] = make(2, chunks[2])
    made[1].wait_recv()
    attend(kv_far[1], positions(chunks[1]) + (1 - core) * 16)
    attend(kv[2], positions(chunks[2]) + core * 16)
    arrive(far)
    made[3] = make(3, chunks[3])
    made[2].wait_recv()
    attend(kv_far[2], positions(chunks[2]) + (1 - core) * 16)
    attend(kv[3], positions(chunks[3]) + core * 16)
    made[3].wait_recv()
    attend(kv_far[3], positions(chunks[3]) + (1 - core) * 16)

    heads = []
    for h in range(2):
        ln[h] = jnp.broadcast_to(top[h] + jnp.log(tot[h]), (8, 256))
        heads.append(acc[h] / tot[h])
    ln_copy = send(ln.at[1 - core], ln_far, PARTNER)
    rows = split(jnp.concatenate(heads, axis=0).T)

    on_z = ((zm, z0, zp, zo), Z_DOWN, Z_UP, Z_OPP)
    on_y = ((ym, y0, yp, yo), Y_DOWN, Y_UP, Y_OPP)
    axes = (on_z, on_y)

    def order(p):
        vm, v0, vp, vo = axes[1 - p][0]
        return vo, vm, vp, v0

    def rows_of(p, u, i, h):
        cols = pl.ds(p * HALF, HALF)
        v = order(p)[i]
        return part.at[v, u, h, :, cols] if p == 0 else part.at[u, v, h, :, cols]

    relays, direct, second, final2 = {}, {}, {}, {}

    def send_direct(p, i):
        (um, u0, up, uo), down, upward, _ = axes[p]
        direct[p, i] = (
            send(rows_of(p, up, i, 1), sums.at[p, 0, i, 1], upward),
            send(rows_of(p, um, i, 0), sums.at[p, 1, i, 0], down),
        )

    for p in range(2):
        (um, u0, up, uo), down, upward, _ = axes[p]
        tile = HALF // 3
        for t in range(3):
            cols = pl.ds(p * HALF + t * tile, tile)
            part[:, :, :, :, cols] = dot3(rows, (woh[:, cols], wol[:, cols])).reshape(4, 4, 2, 8, tile)
        for i in range(4):
            relays[p, i] = (
                send(rows_of(p, uo, i, 0), relay.at[p, 0, i], upward),
                send(rows_of(p, uo, i, 1), relay.at[p, 1, i], down),
            )
        for i in range(2):
            send_direct(p, i)

    def pass_on(p, i):
        (um, u0, up, uo), down, upward, _ = axes[p]
        relays[p, i][0].wait_recv()
        rows_of(p, up, i, 0)[...] += relay[p, 0, i]
        one = send(rows_of(p, up, i, 0), sums.at[p, 0, i, 0], upward)
        relays[p, i][1].wait_recv()
        rows_of(p, um, i, 1)[...] += relay[p, 1, i]
        second[p, i] = (one, send(rows_of(p, um, i, 1), sums.at[p, 1, i, 1], down))

    def finish(p, i):
        u0 = axes[p][0][1]
        _, down, upward, opposite = axes[1 - p]
        for copy in (*direct[p, i], *second[p, i]):
            copy.wait_recv()
        for h in range(2):
            red[p, i, h] = rows_of(p, u0, i, h)[...] + (sums[p, 0, i, h] + sums[p, 1, i, h])
        if i < 3:
            device = (opposite, down, upward)[i]
            final2[p, i] = send(red.at[p, i], sums2.at[p, i], device)

    for i in range(4):
        for p in range(2):
            pass_on(p, i)
            if i < 2:
                send_direct(p, i + 2)
    for i in range(4):
        for p in range(2):
            finish(p, i)

    ln_copy.wait_recv()
    from_lane = lax.broadcasted_iota(jnp.int32, (256, 512), 0)
    to_lane = lax.broadcasted_iota(jnp.int32, (256, 512), 1)
    to_own = lax.div(from_lane, 16) * 32 + lax.rem(from_lane, 16)
    placed = jnp.zeros((8, 512), f32)
    for value, side in ((ln[core], core), (ln_far[...], 1 - core)):
        place = jnp.where(to_lane == to_own + side * 16, 1.0, 0.0).astype(bf16)
        high, rest = value.astype(bf16), value
        rest = rest - high.astype(f32)
        middle = rest.astype(bf16)
        lowest = (rest - middle.astype(f32)).astype(bf16)
        placed = placed + ((dot(high, place) + dot(middle, place)) + dot(lowest, place))
    ln_row[...] = placed[:1]
    stores = [load(ln_row, ln_out)]

    for p in range(2):
        for i in range(3):
            final2[p, i].wait_recv()
        total = red[p, 3] + sums2[p, 0] + (sums2[p, 1] + sums2[p, 2])
        rows_out[:, :, pl.ds(p * HALF, HALF)] = total
        cols = pl.ds(p * HALF, HALF)
        stores.append(load(rows_out.at[:, :, cols], out.at[:, :, cols]))
    for copy in stores:
        copy.wait()
    for copy in copies:
        copy.wait_send()


def body(hidden_rows, segment_ids, w_query, w_down, w_up, w_out):
    any_space = pl.BlockSpec(memory_space=pl.ANY)
    out, ln = pl.pallas_call(
        kernel,
        out_shape=(
            jax.ShapeDtypeStruct((2, 8, D), f32),
            jax.ShapeDtypeStruct((1, TOK_CTX), f32),
        ),
        in_specs=[any_space] * 6,
        out_specs=(any_space, any_space),
        scratch_shapes=[
            pltpu.VMEM((4, 4, 2, 8, D), f32),
            pltpu.VMEM((4, 4, 4, 9, 8, 128), f32),
            pltpu.VMEM((2, QK, D), f32),
            pltpu.VMEM((KV_RANK + ROPE, D), f32),
            pltpu.VMEM((2, KV_RANK, 256), f32),
            pltpu.VMEM((2, VDIM, D), f32),
            pltpu.VMEM((2, QK, D), bf16),
            pltpu.VMEM((2, QK, D), bf16),
            pltpu.VMEM((2, KV_RANK, 256), bf16),
            pltpu.VMEM((2, KV_RANK, 256), bf16),
            pltpu.VMEM((2 * VDIM, D), bf16),
            pltpu.VMEM((2 * VDIM, D), bf16),
            pltpu.VMEM((4, 256, LAT), f32),
            pltpu.VMEM((4, 256, LAT), f32),
            pltpu.VMEM((2, 256, QK), bf16),
            pltpu.VMEM((2, 256, QK), bf16),
            pltpu.VMEM((2, 256, QK), f32),
            pltpu.VMEM((2, 1, 256), f32),
            pltpu.VMEM((2, 1, 256), f32),
            pltpu.VMEM((2, VDIM, 256), f32),
            pltpu.VMEM((4, 4, 2, 8, D), f32),
            pltpu.VMEM((2, 2, 4, 8, HALF), f32),
            pltpu.VMEM((2, 2, 4, 2, 8, HALF), f32),
            pltpu.VMEM((2, 3, 2, 8, HALF), f32),
            pltpu.VMEM((2, 4, 2, 8, HALF), f32),
            pltpu.VMEM((2, 8, 256), f32),
            pltpu.VMEM((8, 256), f32),
            pltpu.VMEM((16, 128), jnp.int32),
            pltpu.VMEM((1, TOK_CTX), f32),
            pltpu.VMEM((2, 8, D), f32),
            pltpu.VMEM((256, D), bf16),
            pltpu.VMEM((256, D), bf16),
            pltpu.SemaphoreType.DMA((N_SEM,)),
            pltpu.SemaphoreType.DMA((N_SEM,)),
            pltpu.SemaphoreType.DMA((16,)),
        ],
        compiler_params=pltpu.CompilerParams(
            collective_id=0, has_side_effects=True, vmem_limit_bytes=58 * 1024 * 1024
        ),
        name="latent_attention",
    )(
        hidden_rows.reshape(2, 8, D), segment_ids.reshape(16, 128),
        w_query.T, w_down.T, w_up, w_out,
    )
    return out.reshape(16, D), ln


def solution(mesh):
    in_specs = (
        P(("ctx", "head"), None),
        P(),
        P(None, "head"),
        P(),
        P(None, "head"),
        P("head", None),
    )
    out_specs = (P(("ctx", "head"), None), P("head", "ctx"))
    return jax.shard_map(body, mesh=mesh, in_specs=in_specs, out_specs=out_specs, check_vma=False)
```

```python
import functools
import math

import jax
import jax.numpy as jnp
from jax import lax
from jax.experimental import pallas as pl
from jax.experimental.pallas import tpu as pltpu
from jax.sharding import PartitionSpec as P

D = 2304
KV_RANK = 512
NOPE = 128
ROPE = 64
VDIM = 128
QK = NOPE + ROPE
TOK_CTX = 512
LAT = 640
HALF = D // 2

eps_norm = 1e-06
neg_fill = -1e30
f32 = jnp.float32
bf16 = jnp.bfloat16
MESH = pl.DeviceIdType.MESH
N_SEM = 200


def split(value):
    high = value.astype(bf16)
    return high, (value - high.astype(f32)).astype(bf16)


def dot(left, right, dims=((1,), (0,))):
    return lax.dot_general(left, right, (dims, ((), ())), preferred_element_type=f32)


def dot3(left, right, dims=((1,), (0,))):
    (left_high, left_low), (right_high, right_low) = left, right
    small = dot(left_high, right_low, dims) + dot(left_low, right_high, dims)
    return dot(left_high, right_high, dims) + small


def kernel(
    x_in, seg_in, wq_in, wd_in, wu_in, wo_in,
    out, ln_out,
    xs, lat, wq, wd, wu, wo, wqh, wql, wuh, wul, woh, wol, kv, kv_far, qh, ql, accq,
    top, tot, acc, part, relay, sums, sums2, red, ln, ln_far, seg, ln_row, rows_out, xh, xl,
    send_sem, recv_sem, load_sem,
):
    ctx = lax.axis_index("ctx")
    head = lax.axis_index("head")
    core = lax.rem(head, 2)
    z0 = lax.rem(lax.div(head, 2), 4)
    y0 = lax.div(head, 8)

    def at(y, z):
        return (ctx, (y * 4 + z) * 2 + core)

    def turn(i, by):
        return lax.rem(i + by + 4, 4)

    ym, yp, yo = turn(y0, -1), turn(y0, 1), turn(y0, 2)
    zm, zp, zo = turn(z0, -1), turn(z0, 1), turn(z0, 2)
    Y_UP, Y_DOWN = at(yp, z0), at(ym, z0)
    Z_UP, Z_DOWN = at(y0, zp), at(y0, zm)
    Y_OPP, Z_OPP = at(yo, z0), at(y0, zo)
    PARTNER = (ctx, head + 1 - 2 * core)
    X_UP, X_DOWN, X_OPP = [(turn(ctx, by), head) for by in (1, -1, 2)]

    barrier = pltpu.get_barrier_semaphore()
    peers = [Y_UP, Y_DOWN, Z_UP, Z_DOWN, Y_OPP, Z_OPP, PARTNER, X_UP, X_DOWN, X_OPP]
    for peer in peers:
        pl.semaphore_signal(barrier, inc=1, device_id=peer, device_id_type=MESH)

    loads = []

    def load(src, dst):
        copy = pltpu.make_async_copy(src, dst, load_sem.at[len(loads)])
        copy.start()
        loads.append(copy)
        return copy

    load_x = load(x_in, xs.at[y0, z0])
    WD_STEPS = 6
    wd_rows = D // WD_STEPS
    load_wd = [
        load(wd_in.at[:, pl.ds(i * wd_rows, wd_rows)], wd.at[:, pl.ds(i * wd_rows, wd_rows)])
        for i in range(WD_STEPS)
    ]
    load_rest = [
        load(wq_in, wq.at[core]), load(wu_in, wu.at[core]), load(wo_in, wo.at[core]),
        load(seg_in, seg),
    ]
    copies = []

    def send(src, dst, device):
        k = len(copies)
        copy = pltpu.make_async_remote_copy(
            src_ref=src, dst_ref=dst, send_sem=send_sem.at[k], recv_sem=recv_sem.at[k],
            device_id=device, device_id_type=MESH,
        )
        copy.start()
        copies.append(copy)
        return copy

    def gather(view, own=None):
        def hand(y, z, p, h, device):
            return send(view(y, z, p, h), view(y, z, p, h), device)

        first = view(y0, z0, None, None) if own is None else own
        target = view(y0, z0, None, None)
        near = [send(first, target, device) for device in (Y_UP, Z_UP, Y_DOWN, Z_DOWN)]
        yield
        near += [send(first, target, device) for device in (Y_OPP, Z_OPP)]
        yield
        a, b = [], []
        for k, i, j in ((0, ym, zm), (2, yp, zp)):
            near[k].wait_recv()
            a += [hand(i, z0, 0, None, Z_UP), hand(i, z0, 0, None, Z_DOWN)]
            near[k + 1].wait_recv()
            b += [hand(y0, j, 1, None, Y_UP), hand(y0, j, 1, None, Y_DOWN)]
        yield
        near[4].wait_recv()
        a += [hand(yo, z0, 0, None, Z_UP), hand(yo, z0, 0, None, Z_DOWN)]
        near[5].wait_recv()
        b += [hand(y0, zo, 1, None, Y_UP), hand(y0, zo, 1, None, Y_DOWN)]
        yield
        last = []
        for i, (y, z) in enumerate(((ym, zm), (yp, zp), (yo, zo))):
            a[2 * i].wait_recv()
            last.append(hand(y, zm, 0, 0, Z_UP))
            b[2 * i].wait_recv()
            last.append(hand(ym, z, 1, 0, Y_UP))
            a[2 * i + 1].wait_recv()
            last.append(hand(y, zp, 0, 1, Z_DOWN))
            b[2 * i + 1].wait_recv()
            last.append(hand(yp, z, 1, 1, Y_DOWN))
            if i:
                yield
        for copy in last:
            copy.wait_recv()
        yield

    everything = slice(None)

    def x_view(y, z, p, h):
        cols = everything if p is None else pl.ds(p * HALF, HALF)
        return xs.at[y, z, :, :, cols] if h is None else xs.at[y, z, h, :, cols]

    def gather_small(slot, neighbours=False):
        def whole(y, z):
            return lat.at[y, z, slot]

        def some(y, z, p):
            return lat.at[y, z, slot, (pl.ds(0, 4), pl.ds(4, 5))[p]]

        passed = {}

        def pass_on(y, z, name):
            if neighbours:
                passed[name] = (
                    send(whole(y, z), lat.at[y, z, 2], X_UP),
                    send(whole(y, z), lat.at[y, z, 3], X_DOWN),
                )

        to_y, to_z = (Y_UP, Y_DOWN, Y_OPP), (Z_UP, Z_DOWN, Z_OPP)
        from_y, from_z = (ym, yp, yo), (zm, zp, zo)
        on_y, on_z = [], []
        for k in range(3):
            on_y.append(send(whole(y0, z0), whole(y0, z0), to_y[k]))
            on_z.append(send(whole(y0, z0), whole(y0, z0), to_z[k]))
        pass_on(y0, z0, "own")
        yield passed
        a, b = {}, {}
        for k in range(3):
            on_y[k].wait_recv()
            for j in range(3):
                a[k, j] = send(some(from_y[k], z0, 0), some(from_y[k], z0, 0), to_z[j])
            on_z[k].wait_recv()
            for j in range(3):
                b[j, k] = send(some(y0, from_z[k], 1), some(y0, from_z[k], 1), to_y[j])
            pass_on(from_y[k], z0, ("y", k))
            pass_on(y0, from_z[k], ("z", k))
        yield passed
        for j in range(3):
            for k in range(3):
                a[k, j].wait_recv()
                b[k, j].wait_recv()
                pass_on(from_y[k], from_z[j], (k, j))
        yield passed

    def make(g, pieces):
        def columns(tiles):
            taken = [
                lat[:, :, slot, tiles] if z is None else lat[:, z, slot, tiles]
                for slot, z in pieces
            ]
            return jnp.concatenate([value.reshape(-1, 128) for value in taken], axis=0)

        both = split(jnp.concatenate([columns(pl.ds(2 * j, 2)) for j in range(4)], axis=1))
        for h in range(2):
            kv[g, :, pl.ds(h * 256, 256)] = dot3(both, (wuh[h], wul[h]))
        shared = columns(8).reshape(16, 8, 128)
        shared = jnp.concatenate([shared[:, :, :64], shared[:, :, 64:]], axis=1).reshape(256, 64)
        kv[g, :, pl.ds(512, 64)] = shared
        kv[g, :, pl.ds(576, 64)] = jnp.zeros((256, 64), f32)
        return send(kv.at[g], kv_far.at[g], PARTNER)

    gather_x = gather(x_view, x_in)

    load_x.wait()
    own_high, own_low = split(xs[y0, z0].reshape(16, D))
    own_both = jnp.concatenate([own_high, own_low], axis=0)
    raw2 = jnp.zeros((32, KV_RANK + ROPE), f32)
    raw1 = jnp.zeros((16, KV_RANK + ROPE), f32)
    for i in range(WD_STEPS):
        load_wd[i].wait()
        w_high, w_low = split(wd[:, pl.ds(i * wd_rows, wd_rows)])
        cols = slice(i * wd_rows, (i + 1) * wd_rows)
        raw2 = raw2 + dot(own_both[:, cols], w_high, ((1,), (1,)))
        raw1 = raw1 + dot(own_high[:, cols], w_low, ((1,), (1,)))
        if i == 0:
            pl.semaphore_wait(barrier, len(peers))
            next(gather_x)
            weight_copies = [
                send(wq_in, wq.at[core], PARTNER),
                send(wu_in, wu.at[core], PARTNER),
                send(wo_in, wo.at[core], PARTNER),
            ]
    raw = raw2[:16] + (raw2[16:] + raw1)
    squeezed = raw[:, :KV_RANK]
    mean_square = jnp.mean(squeezed * squeezed, axis=1, keepdims=True)
    squeezed = squeezed * lax.rsqrt(mean_square + eps_norm)
    for j in range(4):
        tiles = squeezed[:, j * 128 : (j + 1) * 128].reshape(2, 8, 128)
        lat[y0, z0, 0, pl.ds(2 * j, 2)] = tiles
    lat[y0, z0, 0, 8] = jnp.concatenate([raw[:8, KV_RANK:], raw[8:, KV_RANK:]], axis=1)

    across = send(lat.at[y0, z0, 0], lat.at[y0, z0, 1], X_OPP)
    gather_own = gather_small(0, neighbours=True)
    gather_opp = gather_small(1)
    passed = next(gather_own)
    next(gather_x)
    for copy in load_rest:
        copy.wait()
    for copy in weight_copies:
        copy.wait_recv()
    for h in range(2):
        wqh[h], wql[h] = split(wq[h])
    next(gather_x)
    next(gather_own)
    next(gather_x)
    across.wait_recv()
    next(gather_opp)
    next(gather_x)
    for h in range(2):
        wuh[h], wul[h] = split(wu[h])
    next(gather_own)
    made = {0: make(0, [(0, None)])}
    next(gather_x)
    next(gather_opp)
    woh[...], wol[...] = split(wo[...].reshape(2 * VDIM, D))
    next(gather_x)

    accq[...] = jnp.zeros_like(accq)
    xh[...], xl[...] = split(xs[...].reshape(256, D))
    for h in range(2):
        accq[h] = dot3((xh[...], xl[...]), (wqh[h], wql[h]), ((1,), (1,)))

    for h in range(2):
        qh[h], ql[h] = split(accq[h] * (1.0 / math.sqrt(QK)))

    ones = jnp.sum(seg[...], axis=(0, 1), keepdims=True)
    bound = 2048 - ones
    lane = lax.broadcasted_iota(jnp.int32, (1, 256), 1)
    q_pos = ctx * TOK_CTX + lax.div(lane, 16) * 32 + core * 16 + lax.rem(lane, 16)
    q_start = jnp.where(q_pos >= bound, bound, 0)
    row = lax.broadcasted_iota(jnp.int32, (256, 1), 0)
    row_in, row_block = lax.rem(row, 16), lax.div(row, 16)
    slot_ctx = (ctx, turn(ctx, 2), turn(ctx, -1), turn(ctx, 1))

    top[...] = jnp.full_like(top, neg_fill)
    tot[...] = jnp.zeros_like(tot)
    acc[...] = jnp.zeros_like(acc)

    def attend(block, k_pos):
        allowed = (k_pos <= q_pos) & (k_pos >= q_start)
        found, stats = [], []
        for h in range(2):
            keys = jnp.concatenate(
                [block[:, h * 256 : h * 256 + NOPE], block[:, 512 : 512 + ROPE]], axis=1
            )
            scores = dot3(split(keys), (qh[h], ql[h]), ((1,), (1,)))
            found.append(jnp.where(allowed, scores, neg_fill))
        for h in range(2):
            old = top[h]
            new = jnp.maximum(old, jnp.max(found[h], axis=0, keepdims=True))
            weights = jnp.exp(found[h] - new)
            factor = jnp.exp(old - new)
            top[h] = new
            tot[h] = tot[h] * factor + jnp.sum(weights, axis=0, keepdims=True)
            stats.append((factor, split(weights)))
        for h in range(2):
            values = split(block[:, h * 256 + NOPE : (h + 1) * 256].T)
            acc[h] = acc[h] * stats[h][0] + dot3(values, stats[h][1])

    def positions(pieces):
        if len(pieces) == 1:
            at_ctx, block = slot_ctx[pieces[0][0]], row_block
        else:
            pick = lax.div(row, 64)
            at_ctx = jnp.where(pick < 2, slot_ctx[2], slot_ctx[3])
            column = jnp.where(lax.rem(pick, 2) == 0, pieces[0][1], pieces[1][1])
            block = lax.rem(row_block, 4) * 4 + column
        return at_ctx * TOK_CTX + block * 32 + row_in

    def arrive(names):
        for name in names:
            for copy in passed[name]:
                copy.wait_recv()

    chunks = (
        [(0, None)],
        [(1, None)],
        [(2, z0), (2, zm), (3, z0), (3, zm)],
        [(2, zp), (2, zo), (3, zp), (3, zo)],
    )
    near = ["own", ("y", 0), ("y", 1), ("y", 2), ("z", 0), (0, 0), (1, 0), (2, 0)]
    far = [(name, j) for j in (1, 2) for name in ("z", 0, 1, 2)]
    def near_side(g):
        attend(kv[g], positions(chunks[g]) + core * 16)

    def far_side(g):
        made[g].wait_recv()
        attend(kv_far[g], positions(chunks[g]) + (1 - core) * 16)

    near_side(0)
    arrive(near)
    made[2] = make(2, chunks[2])
    far_side(0)
    near_side(2)
    next(gather_opp)
    made[1] = make(1, chunks[1])
    far_side(2)
    near_side(1)
    arrive(far)
    made[3] = make(3, chunks[3])
    far_side(1)
    near_side(3)
    far_side(3)

    gathered = len(copies)
    heads = []
    for h in range(2):
        ln[h] = jnp.broadcast_to(top[h] + jnp.log(tot[h]), (8, 256))
        heads.append(acc[h] / tot[h])
    ln_copy = send(ln.at[1 - core], ln_far, PARTNER)
    rows = split(jnp.concatenate(heads, axis=0).T)

    on_z = ((zm, z0, zp, zo), Z_DOWN, Z_UP, Z_OPP)
    on_y = ((ym, y0, yp, yo), Y_DOWN, Y_UP, Y_OPP)
    axes = (on_z, on_y)

    def order(p):
        vm, v0, vp, vo = axes[1 - p][0]
        return vo, vm, vp, v0

    def rows_of(p, u, i, h):
        cols = pl.ds(p * HALF, HALF)
        v = order(p)[i]
        return part.at[v, u, h, :, cols] if p == 0 else part.at[u, v, h, :, cols]

    relays, direct, second, final2 = {}, {}, {}, {}

    def send_direct(p, i):
        (um, u0, up, uo), down, upward, _ = axes[p]
        direct[p, i] = (
            send(rows_of(p, up, i, 1), sums.at[p, 0, i, 1], upward),
            send(rows_of(p, um, i, 0), sums.at[p, 1, i, 0], down),
        )

    for p in range(2):
        (um, u0, up, uo), down, upward, _ = axes[p]
        tile = HALF // 3
        for t in range(3):
            cols = pl.ds(p * HALF + t * tile, tile)
            part[:, :, :, :, cols] = dot3(rows, (woh[:, cols], wol[:, cols])).reshape(4, 4, 2, 8, tile)
        for i in range(4):
            relays[p, i] = (
                send(rows_of(p, uo, i, 0), relay.at[p, 0, i], upward),
                send(rows_of(p, uo, i, 1), relay.at[p, 1, i], down),
            )
        for i in range(2):
            send_direct(p, i)

    def pass_on(p, i):
        (um, u0, up, uo), down, upward, _ = axes[p]
        relays[p, i][0].wait_recv()
        rows_of(p, up, i, 0)[...] += relay[p, 0, i]
        one = send(rows_of(p, up, i, 0), sums.at[p, 0, i, 0], upward)
        relays[p, i][1].wait_recv()
        rows_of(p, um, i, 1)[...] += relay[p, 1, i]
        second[p, i] = (one, send(rows_of(p, um, i, 1), sums.at[p, 1, i, 1], down))

    def finish(p, i):
        u0 = axes[p][0][1]
        _, down, upward, opposite = axes[1 - p]
        for copy in (*direct[p, i], *second[p, i]):
            copy.wait_recv()
        for h in range(2):
            red[p, i, h] = rows_of(p, u0, i, h)[...] + (sums[p, 0, i, h] + sums[p, 1, i, h])
        if i < 3:
            device = (opposite, down, upward)[i]
            final2[p, i] = send(red.at[p, i], sums2.at[p, i], device)

    for copy in copies[:gathered]:
        copy.wait_send()
    for i in range(4):
        for p in range(2):
            pass_on(p, i)
            if i < 2:
                send_direct(p, i + 2)
    for i in range(4):
        for p in range(2):
            finish(p, i)

    ln_copy.wait_recv()
    from_lane = lax.broadcasted_iota(jnp.int32, (256, 512), 0)
    to_lane = lax.broadcasted_iota(jnp.int32, (256, 512), 1)
    to_own = lax.div(from_lane, 16) * 32 + lax.rem(from_lane, 16)
    placed = jnp.zeros((8, 512), f32)
    for value, side in ((ln[core], core), (ln_far[...], 1 - core)):
        place = jnp.where(to_lane == to_own + side * 16, 1.0, 0.0).astype(bf16)
        high, rest = value.astype(bf16), value
        rest = rest - high.astype(f32)
        middle = rest.astype(bf16)
        lowest = (rest - middle.astype(f32)).astype(bf16)
        placed = placed + ((dot(high, place) + dot(middle, place)) + dot(lowest, place))
    ln_row[...] = placed[:1]
    stores = [load(ln_row, ln_out)]

    for p in range(2):
        for i in range(3):
            final2[p, i].wait_recv()
        total = red[p, 3] + sums2[p, 0] + (sums2[p, 1] + sums2[p, 2])
        rows_out[:, :, pl.ds(p * HALF, HALF)] = total
        cols = pl.ds(p * HALF, HALF)
        stores.append(load(rows_out.at[:, :, cols], out.at[:, :, cols]))
    for copy in stores:
        copy.wait()
    for copy in copies[gathered:]:
        copy.wait_send()


def body(hidden_rows, segment_ids, w_query, w_down, w_up, w_out):
    any_space = pl.BlockSpec(memory_space=pl.ANY)
    out, ln = pl.pallas_call(
        kernel,
        out_shape=(
            jax.ShapeDtypeStruct((2, 8, D), f32),
            jax.ShapeDtypeStruct((1, TOK_CTX), f32),
        ),
        in_specs=[any_space] * 6,
        out_specs=(any_space, any_space),
        scratch_shapes=[
            pltpu.VMEM((4, 4, 2, 8, D), f32),
            pltpu.VMEM((4, 4, 4, 9, 8, 128), f32),
            pltpu.VMEM((2, QK, D), f32),
            pltpu.VMEM((KV_RANK + ROPE, D), f32),
            pltpu.VMEM((2, KV_RANK, 256), f32),
            pltpu.VMEM((2, VDIM, D), f32),
            pltpu.VMEM((2, QK, D), bf16),
            pltpu.VMEM((2, QK, D), bf16),
            pltpu.VMEM((2, KV_RANK, 256), bf16),
            pltpu.VMEM((2, KV_RANK, 256), bf16),
            pltpu.VMEM((2 * VDIM, D), bf16),
            pltpu.VMEM((2 * VDIM, D), bf16),
            pltpu.VMEM((4, 256, LAT), f32),
            pltpu.VMEM((4, 256, LAT), f32),
            pltpu.VMEM((2, 256, QK), bf16),
            pltpu.VMEM((2, 256, QK), bf16),
            pltpu.VMEM((2, 256, QK), f32),
            pltpu.VMEM((2, 1, 256), f32),
            pltpu.VMEM((2, 1, 256), f32),
            pltpu.VMEM((2, VDIM, 256), f32),
            pltpu.VMEM((4, 4, 2, 8, D), f32),
            pltpu.VMEM((2, 2, 4, 8, HALF), f32),
            pltpu.VMEM((2, 2, 4, 2, 8, HALF), f32),
            pltpu.VMEM((2, 3, 2, 8, HALF), f32),
            pltpu.VMEM((2, 4, 2, 8, HALF), f32),
            pltpu.VMEM((2, 8, 256), f32),
            pltpu.VMEM((8, 256), f32),
            pltpu.VMEM((16, 128), jnp.int32),
            pltpu.VMEM((1, TOK_CTX), f32),
            pltpu.VMEM((2, 8, D), f32),
            pltpu.VMEM((256, D), bf16),
            pltpu.VMEM((256, D), bf16),
            pltpu.SemaphoreType.DMA((N_SEM,)),
            pltpu.SemaphoreType.DMA((N_SEM,)),
            pltpu.SemaphoreType.DMA((16,)),
        ],
        compiler_params=pltpu.CompilerParams(
            collective_id=0, has_side_effects=True, vmem_limit_bytes=58 * 1024 * 1024
        ),
        name="latent_attention",
    )(
        hidden_rows.reshape(2, 8, D), segment_ids.reshape(16, 128),
        w_query.T, w_down.T, w_up, w_out,
    )
    return out.reshape(16, D), ln


def solution(mesh):
    in_specs = (
        P(("ctx", "head"), None),
        P(),
        P(None, "head"),
        P(),
        P(None, "head"),
        P("head", None),
    )
    out_specs = (P(("ctx", "head"), None), P("head", "ctx"))
    return jax.shard_map(body, mesh=mesh, in_specs=in_specs, out_specs=out_specs, check_vma=False)
```

```python
import functools
import math

import jax
import jax.numpy as jnp
from jax import lax
from jax.experimental import pallas as pl
from jax.experimental.pallas import tpu as pltpu
from jax.sharding import PartitionSpec as P

D = 2304
KV_RANK = 512
NOPE = 128
ROPE = 64
VDIM = 128
QK = NOPE + ROPE
TOK_CTX = 512
LAT = 640
HALF = D // 2

eps_norm = 1e-06
neg_fill = -1e30
f32 = jnp.float32
bf16 = jnp.bfloat16
MESH = pl.DeviceIdType.MESH
N_SEM = 200


def split(value):
    high = value.astype(bf16)
    return high, (value - high.astype(f32)).astype(bf16)


def dot(left, right, dims=((1,), (0,))):
    return lax.dot_general(left, right, (dims, ((), ())), preferred_element_type=f32)


def dot3(left, right, dims=((1,), (0,))):
    (left_high, left_low), (right_high, right_low) = left, right
    small = dot(left_high, right_low, dims) + dot(left_low, right_high, dims)
    return dot(left_high, right_high, dims) + small


def kernel(
    x_in, seg_in, wq_in, wd_in, wu_in, wo_in,
    out, ln_out,
    xs, lat, wq, wd, wu, wo, wqh, wql, wuh, wul, woh, wol, kv, kv_far, qh, ql, accq,
    top, tot, acc, part, relay, sums, sums2, red, ln, ln_far, seg, ln_row, rows_out, xh, xl,
    send_sem, recv_sem, load_sem,
):
    ctx = lax.axis_index("ctx")
    head = lax.axis_index("head")
    core = lax.rem(head, 2)
    z0 = lax.rem(lax.div(head, 2), 4)
    y0 = lax.div(head, 8)

    def at(y, z):
        return (ctx, (y * 4 + z) * 2 + core)

    def turn(i, by):
        return lax.rem(i + by + 4, 4)

    ym, yp, yo = turn(y0, -1), turn(y0, 1), turn(y0, 2)
    zm, zp, zo = turn(z0, -1), turn(z0, 1), turn(z0, 2)
    Y_UP, Y_DOWN = at(yp, z0), at(ym, z0)
    Z_UP, Z_DOWN = at(y0, zp), at(y0, zm)
    Y_OPP, Z_OPP = at(yo, z0), at(y0, zo)
    PARTNER = (ctx, head + 1 - 2 * core)
    X_UP, X_DOWN, X_OPP = [(turn(ctx, by), head) for by in (1, -1, 2)]

    barrier = pltpu.get_barrier_semaphore()
    peers = [Y_UP, Y_DOWN, Z_UP, Z_DOWN, Y_OPP, Z_OPP, PARTNER, X_UP, X_DOWN, X_OPP]
    for peer in peers:
        pl.semaphore_signal(barrier, inc=1, device_id=peer, device_id_type=MESH)

    loads = []

    def load(src, dst):
        copy = pltpu.make_async_copy(src, dst, load_sem.at[len(loads)])
        copy.start()
        loads.append(copy)
        return copy

    load_x = load(x_in, xs.at[y0, z0])
    WD_STEPS = 6
    wd_rows = D // WD_STEPS
    load_wd = [
        load(wd_in.at[:, pl.ds(i * wd_rows, wd_rows)], wd.at[:, pl.ds(i * wd_rows, wd_rows)])
        for i in range(WD_STEPS)
    ]
    load_rest = [
        load(wq_in, wq.at[core]), load(wu_in, wu.at[core]), load(wo_in, wo.at[core]),
        load(seg_in, seg),
    ]
    copies = []

    def send(src, dst, device):
        k = len(copies)
        copy = pltpu.make_async_remote_copy(
            src_ref=src, dst_ref=dst, send_sem=send_sem.at[k], recv_sem=recv_sem.at[k],
            device_id=device, device_id_type=MESH,
        )
        copy.start()
        copies.append(copy)
        return copy

    def gather(view, own=None):
        def hand(y, z, p, h, device):
            return send(view(y, z, p, h), view(y, z, p, h), device)

        first = view(y0, z0, None, None) if own is None else own
        target = view(y0, z0, None, None)
        near = [send(first, target, device) for device in (Y_UP, Z_UP, Y_DOWN, Z_DOWN)]
        yield
        near += [send(first, target, device) for device in (Y_OPP, Z_OPP)]
        yield
        a, b = [], []
        for k, i, j in ((0, ym, zm), (2, yp, zp)):
            near[k].wait_recv()
            a += [hand(i, z0, 0, None, Z_UP), hand(i, z0, 0, None, Z_DOWN)]
            near[k + 1].wait_recv()
            b += [hand(y0, j, 1, None, Y_UP), hand(y0, j, 1, None, Y_DOWN)]
        yield
        near[4].wait_recv()
        a += [hand(yo, z0, 0, None, Z_UP), hand(yo, z0, 0, None, Z_DOWN)]
        near[5].wait_recv()
        b += [hand(y0, zo, 1, None, Y_UP), hand(y0, zo, 1, None, Y_DOWN)]
        yield
        last = []
        for i, (y, z) in enumerate(((ym, zm), (yp, zp), (yo, zo))):
            a[2 * i].wait_recv()
            last.append(hand(y, zm, 0, 0, Z_UP))
            b[2 * i].wait_recv()
            last.append(hand(ym, z, 1, 0, Y_UP))
            a[2 * i + 1].wait_recv()
            last.append(hand(y, zp, 0, 1, Z_DOWN))
            b[2 * i + 1].wait_recv()
            last.append(hand(yp, z, 1, 1, Y_DOWN))
            if i:
                yield
        for copy in last:
            copy.wait_recv()
        yield

    everything = slice(None)

    def x_view(y, z, p, h):
        cols = everything if p is None else pl.ds(p * HALF, HALF)
        return xs.at[y, z, :, :, cols] if h is None else xs.at[y, z, h, :, cols]

    def gather_small(slot, neighbours=False):
        def whole(y, z):
            return lat.at[y, z, slot]

        def some(y, z, p):
            return lat.at[y, z, slot, (pl.ds(0, 4), pl.ds(4, 5))[p]]

        passed = {}

        def pass_on(y, z, name):
            if neighbours:
                passed[name] = (
                    send(whole(y, z), lat.at[y, z, 2], X_UP),
                    send(whole(y, z), lat.at[y, z, 3], X_DOWN),
                )

        to_y, to_z = (Y_UP, Y_DOWN, Y_OPP), (Z_UP, Z_DOWN, Z_OPP)
        from_y, from_z = (ym, yp, yo), (zm, zp, zo)
        on_y, on_z = [], []
        for k in range(3):
            on_y.append(send(whole(y0, z0), whole(y0, z0), to_y[k]))
            on_z.append(send(whole(y0, z0), whole(y0, z0), to_z[k]))
        pass_on(y0, z0, "own")
        yield passed
        a, b = {}, {}
        for k in range(3):
            on_y[k].wait_recv()
            for j in range(3):
                a[k, j] = send(some(from_y[k], z0, 0), some(from_y[k], z0, 0), to_z[j])
            on_z[k].wait_recv()
            for j in range(3):
                b[j, k] = send(some(y0, from_z[k], 1), some(y0, from_z[k], 1), to_y[j])
            pass_on(from_y[k], z0, ("y", k))
            pass_on(y0, from_z[k], ("z", k))
        yield passed
        for j in range(3):
            for k in range(3):
                a[k, j].wait_recv()
                b[k, j].wait_recv()
                pass_on(from_y[k], from_z[j], (k, j))
        yield passed

    def make(g, pieces):
        def columns(tiles):
            taken = [
                lat[:, :, slot, tiles] if z is None else lat[:, z, slot, tiles]
                for slot, z in pieces
            ]
            return jnp.concatenate([value.reshape(-1, 128) for value in taken], axis=0)

        both = split(jnp.concatenate([columns(pl.ds(2 * j, 2)) for j in range(4)], axis=1))
        for h in range(2):
            kv[g, :, pl.ds(h * 256, 256)] = dot3(both, (wuh[h], wul[h]))
        shared = columns(8).reshape(16, 8, 128)
        shared = jnp.concatenate([shared[:, :, :64], shared[:, :, 64:]], axis=1).reshape(256, 64)
        kv[g, :, pl.ds(512, 64)] = shared
        kv[g, :, pl.ds(576, 64)] = jnp.zeros((256, 64), f32)
        return send(kv.at[g], kv_far.at[g], PARTNER)

    gather_x = gather(x_view, x_in)

    load_x.wait()
    own_high, own_low = split(xs[y0, z0].reshape(16, D))
    own_both = jnp.concatenate([own_high, own_low], axis=0)
    raw2 = jnp.zeros((32, KV_RANK + ROPE), f32)
    raw1 = jnp.zeros((16, KV_RANK + ROPE), f32)
    for i in range(WD_STEPS):
        load_wd[i].wait()
        w_high, w_low = split(wd[:, pl.ds(i * wd_rows, wd_rows)])
        cols = slice(i * wd_rows, (i + 1) * wd_rows)
        raw2 = raw2 + dot(own_both[:, cols], w_high, ((1,), (1,)))
        raw1 = raw1 + dot(own_high[:, cols], w_low, ((1,), (1,)))
        if i == 0:
            pl.semaphore_wait(barrier, len(peers))
            next(gather_x)
            weight_copies = [
                send(wq_in, wq.at[core], PARTNER),
                send(wu_in, wu.at[core], PARTNER),
                send(wo_in, wo.at[core], PARTNER),
            ]
    raw = raw2[:16] + (raw2[16:] + raw1)
    squeezed = raw[:, :KV_RANK]
    mean_square = jnp.mean(squeezed * squeezed, axis=1, keepdims=True)
    squeezed = squeezed * lax.rsqrt(mean_square + eps_norm)
    for j in range(4):
        tiles = squeezed[:, j * 128 : (j + 1) * 128].reshape(2, 8, 128)
        lat[y0, z0, 0, pl.ds(2 * j, 2)] = tiles
    lat[y0, z0, 0, 8] = jnp.concatenate([raw[:8, KV_RANK:], raw[8:, KV_RANK:]], axis=1)

    across = send(lat.at[y0, z0, 0], lat.at[y0, z0, 1], X_OPP)
    gather_own = gather_small(0, neighbours=True)
    gather_opp = gather_small(1)
    passed = next(gather_own)
    next(gather_x)
    for copy in load_rest:
        copy.wait()
    for copy in weight_copies:
        copy.wait_recv()
    for h in range(2):
        wqh[h], wql[h] = split(wq[h])
    next(gather_x)
    next(gather_own)
    next(gather_x)
    across.wait_recv()
    next(gather_opp)
    next(gather_x)
    for h in range(2):
        wuh[h], wul[h] = split(wu[h])
    next(gather_own)
    made = {0: make(0, [(0, None)])}
    next(gather_x)
    next(gather_opp)
    woh[...], wol[...] = split(wo[...].reshape(2 * VDIM, D))
    next(gather_x)

    accq[...] = jnp.zeros_like(accq)
    xh[...], xl[...] = split(xs[...].reshape(256, D))
    for h in range(2):
        accq[h] = dot3((xh[...], xl[...]), (wqh[h], wql[h]), ((1,), (1,)))

    for h in range(2):
        qh[h], ql[h] = split(accq[h] * (1.0 / math.sqrt(QK)))

    ones = jnp.sum(seg[...], axis=(0, 1), keepdims=True)
    bound = 2048 - ones
    lane = lax.broadcasted_iota(jnp.int32, (1, 256), 1)
    q_pos = ctx * TOK_CTX + lax.div(lane, 16) * 32 + core * 16 + lax.rem(lane, 16)
    q_start = jnp.where(q_pos >= bound, bound, 0)
    row = lax.broadcasted_iota(jnp.int32, (256, 1), 0)
    row_in, row_block = lax.rem(row, 16), lax.div(row, 16)
    slot_ctx = (ctx, turn(ctx, 2), turn(ctx, -1), turn(ctx, 1))

    top[...] = jnp.full_like(top, neg_fill)
    tot[...] = jnp.zeros_like(tot)
    acc[...] = jnp.zeros_like(acc)

    def attend(block, k_pos):
        allowed = (k_pos <= q_pos) & (k_pos >= q_start)
        found, stats = [], []
        for h in range(2):
            keys = jnp.concatenate(
                [block[:, h * 256 : h * 256 + NOPE], block[:, 512 : 512 + ROPE]], axis=1
            )
            scores = dot3(split(keys), (qh[h], ql[h]), ((1,), (1,)))
            found.append(jnp.where(allowed, scores, neg_fill))
        for h in range(2):
            old = top[h]
            new = jnp.maximum(old, jnp.max(found[h], axis=0, keepdims=True))
            weights = jnp.exp(found[h] - new)
            factor = jnp.exp(old - new)
            top[h] = new
            tot[h] = tot[h] * factor + jnp.sum(weights, axis=0, keepdims=True)
            stats.append((factor, split(weights)))
        for h in range(2):
            values = split(block[:, h * 256 + NOPE : (h + 1) * 256].T)
            acc[h] = acc[h] * stats[h][0] + dot3(values, stats[h][1])

    def positions(pieces):
        if len(pieces) == 1:
            at_ctx, block = slot_ctx[pieces[0][0]], row_block
        else:
            pick = lax.div(row, 64)
            at_ctx = jnp.where(pick < 2, slot_ctx[2], slot_ctx[3])
            column = jnp.where(lax.rem(pick, 2) == 0, pieces[0][1], pieces[1][1])
            block = lax.rem(row_block, 4) * 4 + column
        return at_ctx * TOK_CTX + block * 32 + row_in

    def arrive(names):
        for name in names:
            for copy in passed[name]:
                copy.wait_recv()

    chunks = (
        [(0, None)],
        [(1, None)],
        [(2, z0), (2, zm), (3, z0), (3, zm)],
        [(2, zp), (2, zo), (3, zp), (3, zo)],
    )
    near = ["own", ("y", 0), ("y", 1), ("y", 2), ("z", 0), (0, 0), (1, 0), (2, 0)]
    far = [(name, j) for j in (1, 2) for name in ("z", 0, 1, 2)]
    def near_side(g):
        return kv[g], positions(chunks[g]) + core * 16

    def far_side(g):
        made[g].wait_recv()
        return kv_far[g], positions(chunks[g]) + (1 - core) * 16

    def attend_both(one, two):
        attend(*(jnp.concatenate(pair, axis=0) for pair in zip(one, two)))

    attend(*near_side(0))
    arrive(near)
    made[2] = make(2, chunks[2])
    attend_both(far_side(0), near_side(2))
    next(gather_opp)
    made[1] = make(1, chunks[1])
    attend_both(far_side(2), near_side(1))
    arrive(far)
    made[3] = make(3, chunks[3])
    attend_both(far_side(1), near_side(3))
    attend(*far_side(3))

    gathered = len(copies)
    heads = []
    for h in range(2):
        ln[h] = jnp.broadcast_to(top[h] + jnp.log(tot[h]), (8, 256))
        heads.append(acc[h] / tot[h])
    ln_copy = send(ln.at[1 - core], ln_far, PARTNER)
    rows = split(jnp.concatenate(heads, axis=0).T)

    on_z = ((zm, z0, zp, zo), Z_DOWN, Z_UP, Z_OPP)
    on_y = ((ym, y0, yp, yo), Y_DOWN, Y_UP, Y_OPP)
    axes = (on_z, on_y)

    def order(p):
        vm, v0, vp, vo = axes[1 - p][0]
        return vo, vm, vp, v0

    def rows_of(p, u, i, h):
        cols = pl.ds(p * HALF, HALF)
        v = order(p)[i]
        return part.at[v, u, h, :, cols] if p == 0 else part.at[u, v, h, :, cols]

    relays, direct, second, final2 = {}, {}, {}, {}

    def send_direct(p, i):
        (um, u0, up, uo), down, upward, _ = axes[p]
        direct[p, i] = (
            send(rows_of(p, up, i, 1), sums.at[p, 0, i, 1], upward),
            send(rows_of(p, um, i, 0), sums.at[p, 1, i, 0], down),
        )

    for p in range(2):
        (um, u0, up, uo), down, upward, _ = axes[p]
        tile = HALF // 3
        for t in range(3):
            cols = pl.ds(p * HALF + t * tile, tile)
            part[:, :, :, :, cols] = dot3(rows, (woh[:, cols], wol[:, cols])).reshape(4, 4, 2, 8, tile)
        for i in range(4):
            relays[p, i] = (
                send(rows_of(p, uo, i, 0), relay.at[p, 0, i], upward),
                send(rows_of(p, uo, i, 1), relay.at[p, 1, i], down),
            )
        for i in range(2):
            send_direct(p, i)

    def pass_on(p, i):
        (um, u0, up, uo), down, upward, _ = axes[p]
        relays[p, i][0].wait_recv()
        rows_of(p, up, i, 0)[...] += relay[p, 0, i]
        one = send(rows_of(p, up, i, 0), sums.at[p, 0, i, 0], upward)
        relays[p, i][1].wait_recv()
        rows_of(p, um, i, 1)[...] += relay[p, 1, i]
        second[p, i] = (one, send(rows_of(p, um, i, 1), sums.at[p, 1, i, 1], down))

    def finish(p, i):
        u0 = axes[p][0][1]
        _, down, upward, opposite = axes[1 - p]
        for copy in (*direct[p, i], *second[p, i]):
            copy.wait_recv()
        for h in range(2):
            red[p, i, h] = rows_of(p, u0, i, h)[...] + (sums[p, 0, i, h] + sums[p, 1, i, h])
        if i < 3:
            device = (opposite, down, upward)[i]
            final2[p, i] = send(red.at[p, i], sums2.at[p, i], device)

    for copy in copies[:gathered]:
        copy.wait_send()
    for i in range(4):
        for p in range(2):
            pass_on(p, i)
            if i < 2:
                send_direct(p, i + 2)
    for i in range(4):
        for p in range(2):
            finish(p, i)

    ln_copy.wait_recv()
    from_lane = lax.broadcasted_iota(jnp.int32, (256, 512), 0)
    to_lane = lax.broadcasted_iota(jnp.int32, (256, 512), 1)
    to_own = lax.div(from_lane, 16) * 32 + lax.rem(from_lane, 16)
    placed = jnp.zeros((8, 512), f32)
    for value, side in ((ln[core], core), (ln_far[...], 1 - core)):
        place = jnp.where(to_lane == to_own + side * 16, 1.0, 0.0).astype(bf16)
        high, rest = value.astype(bf16), value
        rest = rest - high.astype(f32)
        middle = rest.astype(bf16)
        lowest = (rest - middle.astype(f32)).astype(bf16)
        placed = placed + ((dot(high, place) + dot(middle, place)) + dot(lowest, place))
    ln_row[...] = placed[:1]
    stores = [load(ln_row, ln_out)]

    for p in range(2):
        for i in range(3):
            final2[p, i].wait_recv()
        total = red[p, 3] + sums2[p, 0] + (sums2[p, 1] + sums2[p, 2])
        rows_out[:, :, pl.ds(p * HALF, HALF)] = total
        cols = pl.ds(p * HALF, HALF)
        stores.append(load(rows_out.at[:, :, cols], out.at[:, :, cols]))
    for copy in stores:
        copy.wait()
    for copy in copies[gathered:]:
        copy.wait_send()


def body(hidden_rows, segment_ids, w_query, w_down, w_up, w_out):
    any_space = pl.BlockSpec(memory_space=pl.ANY)
    out, ln = pl.pallas_call(
        kernel,
        out_shape=(
            jax.ShapeDtypeStruct((2, 8, D), f32),
            jax.ShapeDtypeStruct((1, TOK_CTX), f32),
        ),
        in_specs=[any_space] * 6,
        out_specs=(any_space, any_space),
        scratch_shapes=[
            pltpu.VMEM((4, 4, 2, 8, D), f32),
            pltpu.VMEM((4, 4, 4, 9, 8, 128), f32),
            pltpu.VMEM((2, QK, D), f32),
            pltpu.VMEM((KV_RANK + ROPE, D), f32),
            pltpu.VMEM((2, KV_RANK, 256), f32),
            pltpu.VMEM((2, VDIM, D), f32),
            pltpu.VMEM((2, QK, D), bf16),
            pltpu.VMEM((2, QK, D), bf16),
            pltpu.VMEM((2, KV_RANK, 256), bf16),
            pltpu.VMEM((2, KV_RANK, 256), bf16),
            pltpu.VMEM((2 * VDIM, D), bf16),
            pltpu.VMEM((2 * VDIM, D), bf16),
            pltpu.VMEM((4, 256, LAT), f32),
            pltpu.VMEM((4, 256, LAT), f32),
            pltpu.VMEM((2, 256, QK), bf16),
            pltpu.VMEM((2, 256, QK), bf16),
            pltpu.VMEM((2, 256, QK), f32),
            pltpu.VMEM((2, 1, 256), f32),
            pltpu.VMEM((2, 1, 256), f32),
            pltpu.VMEM((2, VDIM, 256), f32),
            pltpu.VMEM((4, 4, 2, 8, D), f32),
            pltpu.VMEM((2, 2, 4, 8, HALF), f32),
            pltpu.VMEM((2, 2, 4, 2, 8, HALF), f32),
            pltpu.VMEM((2, 3, 2, 8, HALF), f32),
            pltpu.VMEM((2, 4, 2, 8, HALF), f32),
            pltpu.VMEM((2, 8, 256), f32),
            pltpu.VMEM((8, 256), f32),
            pltpu.VMEM((16, 128), jnp.int32),
            pltpu.VMEM((1, TOK_CTX), f32),
            pltpu.VMEM((2, 8, D), f32),
            pltpu.VMEM((256, D), bf16),
            pltpu.VMEM((256, D), bf16),
            pltpu.SemaphoreType.DMA((N_SEM,)),
            pltpu.SemaphoreType.DMA((N_SEM,)),
            pltpu.SemaphoreType.DMA((16,)),
        ],
        compiler_params=pltpu.CompilerParams(
            collective_id=0, has_side_effects=True, vmem_limit_bytes=58 * 1024 * 1024
        ),
        name="latent_attention",
    )(
        hidden_rows.reshape(2, 8, D), segment_ids.reshape(16, 128),
        w_query.T, w_down.T, w_up, w_out,
    )
    return out.reshape(16, D), ln


def solution(mesh):
    in_specs = (
        P(("ctx", "head"), None),
        P(),
        P(None, "head"),
        P(),
        P(None, "head"),
        P("head", None),
    )
    out_specs = (P(("ctx", "head"), None), P("head", "ctx"))
    return jax.shard_map(body, mesh=mesh, in_specs=in_specs, out_specs=out_specs, check_vma=False)
```

```python
import functools
import math

import jax
import jax.numpy as jnp
from jax import lax
from jax.experimental import pallas as pl
from jax.experimental.pallas import tpu as pltpu
from jax.sharding import PartitionSpec as P

D = 2304
KV_RANK = 512
NOPE = 128
ROPE = 64
VDIM = 128
QK = NOPE + ROPE
TOK_CTX = 512
LAT = 640
HALF = D // 2

eps_norm = 1e-06
neg_fill = -1e30
f32 = jnp.float32
bf16 = jnp.bfloat16
MESH = pl.DeviceIdType.MESH
N_SEM = 200


def split(value):
    high = value.astype(bf16)
    return high, (value - high.astype(f32)).astype(bf16)


def dot(left, right, dims=((1,), (0,))):
    return lax.dot_general(left, right, (dims, ((), ())), preferred_element_type=f32)


def dot3(left, right, dims=((1,), (0,))):
    (left_high, left_low), (right_high, right_low) = left, right
    small = dot(left_high, right_low, dims) + dot(left_low, right_high, dims)
    return dot(left_high, right_high, dims) + small


def kernel(
    x_in, seg_in, wq_in, wd_in, wu_in, wo_in,
    out, ln_out,
    xs, lat, wq, wd, wu, wo, wqh, wql, wuh, wul, woh, wol, kv, kv_far, qh, ql, accq,
    top, tot, acc, part, relay, sums, sums2, red, ln, ln_far, seg, ln_row, rows_out, xh, xl,
    send_sem, recv_sem, load_sem,
):
    ctx = lax.axis_index("ctx")
    head = lax.axis_index("head")
    core = lax.rem(head, 2)
    z0 = lax.rem(lax.div(head, 2), 4)
    y0 = lax.div(head, 8)

    def at(y, z):
        return (ctx, (y * 4 + z) * 2 + core)

    def turn(i, by):
        return lax.rem(i + by + 4, 4)

    ym, yp, yo = turn(y0, -1), turn(y0, 1), turn(y0, 2)
    zm, zp, zo = turn(z0, -1), turn(z0, 1), turn(z0, 2)
    Y_UP, Y_DOWN = at(yp, z0), at(ym, z0)
    Z_UP, Z_DOWN = at(y0, zp), at(y0, zm)
    Y_OPP, Z_OPP = at(yo, z0), at(y0, zo)
    PARTNER = (ctx, head + 1 - 2 * core)
    X_UP, X_DOWN, X_OPP = [(turn(ctx, by), head) for by in (1, -1, 2)]

    barrier = pltpu.get_barrier_semaphore()
    peers = [Y_UP, Y_DOWN, Z_UP, Z_DOWN, Y_OPP, Z_OPP, PARTNER, X_UP, X_DOWN, X_OPP]
    for peer in peers:
        pl.semaphore_signal(barrier, inc=1, device_id=peer, device_id_type=MESH)

    loads = []

    def load(src, dst):
        copy = pltpu.make_async_copy(src, dst, load_sem.at[len(loads)])
        copy.start()
        loads.append(copy)
        return copy

    load_x = load(x_in, xs.at[y0, z0])
    WD_STEPS = 6
    wd_rows = D // WD_STEPS
    load_wd = [
        load(wd_in.at[:, pl.ds(i * wd_rows, wd_rows)], wd.at[:, pl.ds(i * wd_rows, wd_rows)])
        for i in range(WD_STEPS)
    ]
    load_rest = [
        load(wq_in, wq.at[core]), load(wu_in, wu.at[core]), load(wo_in, wo.at[core]),
        load(seg_in, seg),
    ]
    copies = []

    def send(src, dst, device):
        k = len(copies)
        copy = pltpu.make_async_remote_copy(
            src_ref=src, dst_ref=dst, send_sem=send_sem.at[k], recv_sem=recv_sem.at[k],
            device_id=device, device_id_type=MESH,
        )
        copy.start()
        copies.append(copy)
        return copy

    def gather(view, own=None):
        def hand(y, z, p, h, device):
            return send(view(y, z, p, h), view(y, z, p, h), device)

        first = view(y0, z0, None, None) if own is None else own
        target = view(y0, z0, None, None)
        near = [send(first, target, device) for device in (Y_UP, Z_UP, Y_DOWN, Z_DOWN)]
        yield
        near += [send(first, target, device) for device in (Y_OPP, Z_OPP)]
        yield
        a, b = [], []
        for k, i, j in ((0, ym, zm), (2, yp, zp)):
            near[k].wait_recv()
            a += [hand(i, z0, 0, None, Z_UP), hand(i, z0, 0, None, Z_DOWN)]
            near[k + 1].wait_recv()
            b += [hand(y0, j, 1, None, Y_UP), hand(y0, j, 1, None, Y_DOWN)]
        yield
        near[4].wait_recv()
        a += [hand(yo, z0, 0, None, Z_UP), hand(yo, z0, 0, None, Z_DOWN)]
        near[5].wait_recv()
        b += [hand(y0, zo, 1, None, Y_UP), hand(y0, zo, 1, None, Y_DOWN)]
        yield
        last = []
        for i, (y, z) in enumerate(((ym, zm), (yp, zp), (yo, zo))):
            a[2 * i].wait_recv()
            last.append(hand(y, zm, 0, 0, Z_UP))
            b[2 * i].wait_recv()
            last.append(hand(ym, z, 1, 0, Y_UP))
            a[2 * i + 1].wait_recv()
            last.append(hand(y, zp, 0, 1, Z_DOWN))
            b[2 * i + 1].wait_recv()
            last.append(hand(yp, z, 1, 1, Y_DOWN))
            if i:
                yield
        for copy in last:
            copy.wait_recv()
        yield

    everything = slice(None)

    def x_view(y, z, p, h):
        cols = everything if p is None else pl.ds(p * HALF, HALF)
        return xs.at[y, z, :, :, cols] if h is None else xs.at[y, z, h, :, cols]

    def gather_small(slot, neighbours=False):
        def whole(y, z):
            return lat.at[y, z, slot]

        def some(y, z, p):
            return lat.at[y, z, slot, (pl.ds(0, 4), pl.ds(4, 5))[p]]

        passed = {}

        def pass_on(y, z, name):
            if neighbours:
                passed[name] = (
                    send(whole(y, z), lat.at[y, z, 2], X_UP),
                    send(whole(y, z), lat.at[y, z, 3], X_DOWN),
                )

        to_y, to_z = (Y_UP, Y_DOWN, Y_OPP), (Z_UP, Z_DOWN, Z_OPP)
        from_y, from_z = (ym, yp, yo), (zm, zp, zo)
        on_y, on_z = [], []
        for k in range(3):
            on_y.append(send(whole(y0, z0), whole(y0, z0), to_y[k]))
            on_z.append(send(whole(y0, z0), whole(y0, z0), to_z[k]))
        pass_on(y0, z0, "own")
        yield passed
        a, b = {}, {}
        for k in range(3):
            on_y[k].wait_recv()
            for j in range(3):
                a[k, j] = send(some(from_y[k], z0, 0), some(from_y[k], z0, 0), to_z[j])
            on_z[k].wait_recv()
            for j in range(3):
                b[j, k] = send(some(y0, from_z[k], 1), some(y0, from_z[k], 1), to_y[j])
            pass_on(from_y[k], z0, ("y", k))
            pass_on(y0, from_z[k], ("z", k))
        yield passed
        for j in range(3):
            for k in range(3):
                a[k, j].wait_recv()
                b[k, j].wait_recv()
                pass_on(from_y[k], from_z[j], (k, j))
        yield passed

    def make(g, pieces):
        def columns(tiles):
            taken = [
                lat[:, :, slot, tiles] if z is None else lat[:, z, slot, tiles]
                for slot, z in pieces
            ]
            return jnp.concatenate([value.reshape(-1, 128) for value in taken], axis=0)

        both = split(jnp.concatenate([columns(pl.ds(2 * j, 2)) for j in range(4)], axis=1))
        for h in range(2):
            kv[g, :, pl.ds(h * 256, 256)] = dot3(both, (wuh[h], wul[h]))
        shared = columns(8).reshape(16, 8, 128)
        shared = jnp.concatenate([shared[:, :, :64], shared[:, :, 64:]], axis=1).reshape(256, 64)
        kv[g, :, pl.ds(512, 64)] = shared
        kv[g, :, pl.ds(576, 64)] = jnp.zeros((256, 64), f32)
        return send(kv.at[g], kv_far.at[g], PARTNER)

    gather_x = gather(x_view, x_in)

    load_x.wait()
    own_high, own_low = split(xs[y0, z0].reshape(16, D))
    own_both = jnp.concatenate([own_high, own_low], axis=0)
    raw2 = jnp.zeros((32, KV_RANK + ROPE), f32)
    raw1 = jnp.zeros((16, KV_RANK + ROPE), f32)
    for i in range(WD_STEPS):
        load_wd[i].wait()
        w_high, w_low = split(wd[:, pl.ds(i * wd_rows, wd_rows)])
        cols = slice(i * wd_rows, (i + 1) * wd_rows)
        raw2 = raw2 + dot(own_both[:, cols], w_high, ((1,), (1,)))
        raw1 = raw1 + dot(own_high[:, cols], w_low, ((1,), (1,)))
        if i == 0:
            pl.semaphore_wait(barrier, len(peers))
            next(gather_x)
            weight_copies = [
                send(wq_in, wq.at[core], PARTNER),
                send(wu_in, wu.at[core], PARTNER),
                send(wo_in, wo.at[core], PARTNER),
            ]
    raw = raw2[:16] + (raw2[16:] + raw1)
    squeezed = raw[:, :KV_RANK]
    mean_square = jnp.mean(squeezed * squeezed, axis=1, keepdims=True)
    squeezed = squeezed * lax.rsqrt(mean_square + eps_norm)
    for j in range(4):
        tiles = squeezed[:, j * 128 : (j + 1) * 128].reshape(2, 8, 128)
        lat[y0, z0, 0, pl.ds(2 * j, 2)] = tiles
    lat[y0, z0, 0, 8] = jnp.concatenate([raw[:8, KV_RANK:], raw[8:, KV_RANK:]], axis=1)

    across = send(lat.at[y0, z0, 0], lat.at[y0, z0, 1], X_OPP)
    gather_own = gather_small(0, neighbours=True)
    gather_opp = gather_small(1)
    passed = next(gather_own)
    next(gather_x)
    for copy in load_rest:
        copy.wait()
    for copy in weight_copies:
        copy.wait_recv()
    for h in range(2):
        wqh[h], wql[h] = split(wq[h])
    next(gather_x)
    next(gather_own)
    next(gather_x)
    across.wait_recv()
    next(gather_opp)
    next(gather_x)
    for h in range(2):
        wuh[h], wul[h] = split(wu[h])
    next(gather_own)
    made = {0: make(0, [(0, None)])}
    next(gather_x)
    next(gather_opp)
    woh[...], wol[...] = split(wo[...].reshape(2 * VDIM, D))
    next(gather_x)

    accq[...] = jnp.zeros_like(accq)
    xh[...], xl[...] = split(xs[...].reshape(256, D))
    for h in range(2):
        accq[h] = dot3((xh[...], xl[...]), (wqh[h], wql[h]), ((1,), (1,)))

    for h in range(2):
        qh[h], ql[h] = split(accq[h] * (1.0 / math.sqrt(QK)))

    ones = jnp.sum(seg[...], axis=(0, 1), keepdims=True)
    bound = 2048 - ones
    lane = lax.broadcasted_iota(jnp.int32, (1, 256), 1)
    q_pos = ctx * TOK_CTX + lax.div(lane, 16) * 32 + core * 16 + lax.rem(lane, 16)
    q_start = jnp.where(q_pos >= bound, bound, 0)
    row = lax.broadcasted_iota(jnp.int32, (256, 1), 0)
    row_in, row_block = lax.rem(row, 16), lax.div(row, 16)
    slot_ctx = (ctx, turn(ctx, 2), turn(ctx, -1), turn(ctx, 1))

    top[...] = jnp.full_like(top, neg_fill)
    tot[...] = jnp.zeros_like(tot)
    acc[...] = jnp.zeros_like(acc)

    def attend(block, k_pos):
        allowed = (k_pos <= q_pos) & (k_pos >= q_start)
        found, stats = [], []
        for h in range(2):
            keys = jnp.concatenate(
                [block[:, h * 256 : h * 256 + NOPE], block[:, 512 : 512 + ROPE]], axis=1
            )
            scores = dot3(split(keys), (qh[h], ql[h]), ((1,), (1,)))
            found.append(jnp.where(allowed, scores, neg_fill))
        for h in range(2):
            old = top[h]
            new = jnp.maximum(old, jnp.max(found[h], axis=0, keepdims=True))
            weights = jnp.exp(found[h] - new)
            factor = jnp.exp(old - new)
            top[h] = new
            tot[h] = tot[h] * factor + jnp.sum(weights, axis=0, keepdims=True)
            stats.append((factor, split(weights)))
        for h in range(2):
            values = split(block[:, h * 256 + NOPE : (h + 1) * 256].T)
            acc[h] = acc[h] * stats[h][0] + dot3(values, stats[h][1])

    def positions(pieces):
        if len(pieces) == 1:
            at_ctx, block = slot_ctx[pieces[0][0]], row_block
        else:
            pick = lax.div(row, 64)
            at_ctx = jnp.where(pick < 2, slot_ctx[2], slot_ctx[3])
            column = jnp.where(lax.rem(pick, 2) == 0, pieces[0][1], pieces[1][1])
            block = lax.rem(row_block, 4) * 4 + column
        return at_ctx * TOK_CTX + block * 32 + row_in

    def arrive(names):
        for name in names:
            for copy in passed[name]:
                copy.wait_recv()

    chunks = (
        [(0, None)],
        [(1, None)],
        [(2, z0), (2, zm), (3, z0), (3, zm)],
        [(2, zp), (2, zo), (3, zp), (3, zo)],
    )
    near = ["own", ("y", 0), ("y", 1), ("y", 2), ("z", 0), (0, 0), (1, 0), (2, 0)]
    far = [(name, j) for j in (1, 2) for name in ("z", 0, 1, 2)]
    def near_side(g):
        return kv[g], positions(chunks[g]) + core * 16

    def far_side(g):
        made[g].wait_recv()
        return kv_far[g], positions(chunks[g]) + (1 - core) * 16

    def attend_both(one, two):
        attend(*(jnp.concatenate(pair, axis=0) for pair in zip(one, two)))

    attend(*near_side(0))
    arrive(near)
    made[2] = make(2, chunks[2])
    attend_both(far_side(0), near_side(2))
    next(gather_opp)
    made[1] = make(1, chunks[1])
    attend_both(far_side(2), near_side(1))
    arrive(far)
    made[3] = make(3, chunks[3])
    attend_both(far_side(1), near_side(3))
    attend(*far_side(3))

    gathered = len(copies)
    heads = []
    for h in range(2):
        ln[h] = jnp.broadcast_to(top[h] + jnp.log(tot[h]), (8, 256))
        heads.append(acc[h] / tot[h])
    ln_copy = send(ln.at[1 - core], ln_far, PARTNER)
    rows = split(jnp.concatenate(heads, axis=0).T)

    on_z = ((zm, z0, zp, zo), Z_DOWN, Z_UP, Z_OPP)
    on_y = ((ym, y0, yp, yo), Y_DOWN, Y_UP, Y_OPP)
    axes = (on_z, on_y)

    def order(p):
        vm, v0, vp, vo = axes[1 - p][0]
        return vo, vm, vp, v0

    def rows_of(p, u, i, h):
        cols = pl.ds(p * HALF, HALF)
        v = order(p)[i]
        return part.at[v, u, h, :, cols] if p == 0 else part.at[u, v, h, :, cols]

    relays, direct, second, final2 = {}, {}, {}, {}

    def send_direct(p, i):
        (um, u0, up, uo), down, upward, _ = axes[p]
        direct[p, i] = (
            send(rows_of(p, up, i, 1), sums.at[p, 0, i, 1], upward),
            send(rows_of(p, um, i, 0), sums.at[p, 1, i, 0], down),
        )

    for p in range(2):
        (um, u0, up, uo), down, upward, _ = axes[p]
        tile = HALF
        for t in range(1):
            cols = pl.ds(p * HALF + t * tile, tile)
            part[:, :, :, :, cols] = dot3(rows, (woh[:, cols], wol[:, cols])).reshape(4, 4, 2, 8, tile)
        for i in range(4):
            relays[p, i] = (
                send(rows_of(p, uo, i, 0), relay.at[p, 0, i], upward),
                send(rows_of(p, uo, i, 1), relay.at[p, 1, i], down),
            )
        for i in range(2):
            send_direct(p, i)

    def pass_on(p, i):
        (um, u0, up, uo), down, upward, _ = axes[p]
        relays[p, i][0].wait_recv()
        rows_of(p, up, i, 0)[...] += relay[p, 0, i]
        one = send(rows_of(p, up, i, 0), sums.at[p, 0, i, 0], upward)
        relays[p, i][1].wait_recv()
        rows_of(p, um, i, 1)[...] += relay[p, 1, i]
        second[p, i] = (one, send(rows_of(p, um, i, 1), sums.at[p, 1, i, 1], down))

    def finish(p, i):
        u0 = axes[p][0][1]
        _, down, upward, opposite = axes[1 - p]
        for copy in (*direct[p, i], *second[p, i]):
            copy.wait_recv()
        for h in range(2):
            red[p, i, h] = rows_of(p, u0, i, h)[...] + (sums[p, 0, i, h] + sums[p, 1, i, h])
        if i < 3:
            device = (opposite, down, upward)[i]
            final2[p, i] = send(red.at[p, i], sums2.at[p, i], device)

    for copy in copies[:gathered]:
        copy.wait_send()
    for i in range(4):
        for p in range(2):
            pass_on(p, i)
            if i < 2:
                send_direct(p, i + 2)
    for i in range(4):
        for p in range(2):
            finish(p, i)

    ln_copy.wait_recv()
    from_lane = lax.broadcasted_iota(jnp.int32, (256, 512), 0)
    to_lane = lax.broadcasted_iota(jnp.int32, (256, 512), 1)
    to_own = lax.div(from_lane, 16) * 32 + lax.rem(from_lane, 16)
    placed = jnp.zeros((8, 512), f32)
    for value, side in ((ln[core], core), (ln_far[...], 1 - core)):
        place = jnp.where(to_lane == to_own + side * 16, 1.0, 0.0).astype(bf16)
        high, rest = value.astype(bf16), value
        rest = rest - high.astype(f32)
        middle = rest.astype(bf16)
        lowest = (rest - middle.astype(f32)).astype(bf16)
        placed = placed + ((dot(high, place) + dot(middle, place)) + dot(lowest, place))
    ln_row[...] = placed[:1]
    stores = [load(ln_row, ln_out)]

    for p in range(2):
        for i in range(3):
            final2[p, i].wait_recv()
        total = red[p, 3] + sums2[p, 0] + (sums2[p, 1] + sums2[p, 2])
        rows_out[:, :, pl.ds(p * HALF, HALF)] = total
        cols = pl.ds(p * HALF, HALF)
        stores.append(load(rows_out.at[:, :, cols], out.at[:, :, cols]))
    for copy in stores:
        copy.wait()
    for copy in copies[gathered:]:
        copy.wait_send()


def body(hidden_rows, segment_ids, w_query, w_down, w_up, w_out):
    any_space = pl.BlockSpec(memory_space=pl.ANY)
    out, ln = pl.pallas_call(
        kernel,
        out_shape=(
            jax.ShapeDtypeStruct((2, 8, D), f32),
            jax.ShapeDtypeStruct((1, TOK_CTX), f32),
        ),
        in_specs=[any_space] * 6,
        out_specs=(any_space, any_space),
        scratch_shapes=[
            pltpu.VMEM((4, 4, 2, 8, D), f32),
            pltpu.VMEM((4, 4, 4, 9, 8, 128), f32),
            pltpu.VMEM((2, QK, D), f32),
            pltpu.VMEM((KV_RANK + ROPE, D), f32),
            pltpu.VMEM((2, KV_RANK, 256), f32),
            pltpu.VMEM((2, VDIM, D), f32),
            pltpu.VMEM((2, QK, D), bf16),
            pltpu.VMEM((2, QK, D), bf16),
            pltpu.VMEM((2, KV_RANK, 256), bf16),
            pltpu.VMEM((2, KV_RANK, 256), bf16),
            pltpu.VMEM((2 * VDIM, D), bf16),
            pltpu.VMEM((2 * VDIM, D), bf16),
            pltpu.VMEM((4, 256, LAT), f32),
            pltpu.VMEM((4, 256, LAT), f32),
            pltpu.VMEM((2, 256, QK), bf16),
            pltpu.VMEM((2, 256, QK), bf16),
            pltpu.VMEM((2, 256, QK), f32),
            pltpu.VMEM((2, 1, 256), f32),
            pltpu.VMEM((2, 1, 256), f32),
            pltpu.VMEM((2, VDIM, 256), f32),
            pltpu.VMEM((4, 4, 2, 8, D), f32),
            pltpu.VMEM((2, 2, 4, 8, HALF), f32),
            pltpu.VMEM((2, 2, 4, 2, 8, HALF), f32),
            pltpu.VMEM((2, 3, 2, 8, HALF), f32),
            pltpu.VMEM((2, 4, 2, 8, HALF), f32),
            pltpu.VMEM((2, 8, 256), f32),
            pltpu.VMEM((8, 256), f32),
            pltpu.VMEM((16, 128), jnp.int32),
            pltpu.VMEM((1, TOK_CTX), f32),
            pltpu.VMEM((2, 8, D), f32),
            pltpu.VMEM((256, D), bf16),
            pltpu.VMEM((256, D), bf16),
            pltpu.SemaphoreType.DMA((N_SEM,)),
            pltpu.SemaphoreType.DMA((N_SEM,)),
            pltpu.SemaphoreType.DMA((16,)),
        ],
        compiler_params=pltpu.CompilerParams(
            collective_id=0, has_side_effects=True, vmem_limit_bytes=58 * 1024 * 1024
        ),
        name="latent_attention",
    )(
        hidden_rows.reshape(2, 8, D), segment_ids.reshape(16, 128),
        w_query.T, w_down.T, w_up, w_out,
    )
    return out.reshape(16, D), ln


def solution(mesh):
    in_specs = (
        P(("ctx", "head"), None),
        P(),
        P(None, "head"),
        P(),
        P(None, "head"),
        P("head", None),
    )
    out_specs = (P(("ctx", "head"), None), P("head", "ctx"))
    return jax.shard_map(body, mesh=mesh, in_specs=in_specs, out_specs=out_specs, check_vma=False)
```
